512 devices in a mesh: inp: 128 (over y, z, core), sec: 4 (over x).
Axes of the slice: x: 4, y: 8, z: 8, core: 2. Of those that a mesh axis runs over, the one named last changes fastest.
Arguments:
- samples: bfloat16 [1024, 128, 2048], P('inp', 'sec'), may hold values from -6 to 6
- fir_weights: float32 [4, 2048], replicated, may hold values from -3 to 3
- channel_owner: int32 [768], replicated, may hold values from 0 to 127, as said below
Outputs:
- visibility: bfloat16 [1024, 1024, 1024], P(('inp', 'sec'))
- auto_power: float32 [1024, 1024], P(('inp', 'sec'))
The draws below stay inside these ranges and needn't reach their ends.
Inputs may be any that keep to these rules, and one draw needn't show every extreme that they name: `channel_owner`: no owner is named by more than 8 channels, and some owner is named by exactly 8; counts differ from owner to owner.
All inputs are finite; a program needn't handle non-finite values.
Results may differ from the reference program's by a relative error of at most 0.0076.
Values may be sent and summed in bfloat16 or wider, within the bound.
No kernel may reach another device: no remote copies, remote signals or barrier semaphores. Data moves between devices by JAX's collectives and lax.ppermute only.
A program may use at most 64 MiB of HBM per device.

```python
import math
import jax
import jax.numpy as jnp
from jax import lax

INPUTS = 1024
POINTS = 2048
CHANNELS = 768
TAPS = 4
FRAMES = 128
SLOTS = 8
N_INP = 128


def draw_channel_owner(key, part):
    key = jax.random.fold_in(key, 7)
    key_busy, key_order, key_shuffle = jax.random.split(key, 3)
    slot_total = N_INP * SLOTS
    busiest = jax.random.randint(key_busy, (), 0, N_INP)
    priority = jax.random.permutation(key_order, slot_total)
    slot_index = jnp.arange(slot_total)
    priority = jnp.where(slot_index // SLOTS == busiest, slot_index - slot_total, priority)
    ordering = jnp.argsort(priority, stable=True)
    chosen = ordering[:CHANNELS] // SLOTS
    return jax.random.permutation(key_shuffle, chosen).astype(jnp.int32)


def block_scale(key, shape, pieces, smallest, high):
    def one(axis_at, blocks):
        draws = jax.random.uniform(jax.random.fold_in(jax.random.fold_in(key, 6), axis_at), (blocks,), jnp.float32, smallest / len(pieces), high / len(pieces))
        return jnp.repeat(jnp.exp(draws), shape[axis_at] // blocks).reshape((-1,) + (1,) * (len(shape) - axis_at - 1))

    gain = one(*pieces[0])
    for cut in pieces[1:]:
        gain = gain * one(*cut)
    return gain


def noise(key, shape, width, bound, pieces=(), kind=jnp.bfloat16):
    drawn = jax.random.normal(key, shape, jnp.float32) * width
    if len(pieces) > 0:
        drawn = block_scale(key, shape, pieces, -0.22, 0.18) * drawn
    return jnp.clip(drawn, min=-bound, max=bound).astype(kind)


def setup_inputs(seed: int = 0) -> dict:
    seeds = jax.random.split(jax.random.key(seed), 4)
    return {
        "samples": noise(seeds[0], (INPUTS, FRAMES, POINTS), 1.0, 6.0, ((0, 128), (1, 4))),
        "fir_weights": noise(seeds[1], (TAPS, POINTS), 0.5, 3.0, (), jnp.float32),
        "channel_owner": draw_channel_owner(jax.random.fold_in(seeds[3], 71), 0),
    }


def dft_table():
    sample_index = jnp.arange(POINTS, dtype=jnp.int32)
    channel_bins = jnp.arange(CHANNELS, dtype=jnp.int32)
    phases = sample_index[:, None] * channel_bins[None, :] % POINTS
    angles = phases.astype(jnp.float32) * (2.0 * math.pi / POINTS)
    norm_factor = 1.0 / math.sqrt(POINTS)
    return (jnp.concatenate([jnp.cos(angles), -jnp.sin(angles)], axis=1) * norm_factor).astype(jnp.bfloat16)

def slot_lookup(channel_owner, slot_total, slots_per):
    channel_index = jnp.arange(channel_owner.shape[0], dtype=jnp.int32)
    earlier_same = (channel_owner[:, None] == channel_owner[None, :]) & (channel_index[None, :] < channel_index[:, None])
    slot_rank = lax.optimization_barrier(jnp.sum(earlier_same.astype(jnp.int32), axis=1))
    slot_target = channel_owner * slots_per + slot_rank
    slot_index = jnp.arange(slot_total, dtype=jnp.int32)
    slot_match = (slot_target[None, :] == slot_index[:, None]).astype(jnp.int32)
    channel_id = lax.optimization_barrier(jnp.sum(slot_match * channel_index[None, :], axis=1)).astype(jnp.int32)
    slot_live = lax.optimization_barrier(jnp.sum(slot_match, axis=1)).astype(jnp.int32)
    return (channel_id, slot_live)

def channelize(series, fir_weights, dft_matrix):
    extended = jnp.concatenate([jnp.zeros((TAPS - 1, POINTS), jnp.bfloat16), series], axis=0)
    accumulated = jnp.zeros((FRAMES, POINTS), jnp.float32)
    for tap in range(TAPS):
        offset = TAPS - 1 - tap
        accumulated = accumulated + fir_weights[tap][None, :] * extended[offset:offset + FRAMES].astype(jnp.float32)
    filtered = accumulated.astype(jnp.bfloat16)
    return jnp.dot(filtered, dft_matrix, preferred_element_type=jnp.float32).astype(jnp.bfloat16)

def reference(samples, fir_weights, channel_owner):
    dft_matrix = dft_table()
    spectra = lax.map(lambda series: channelize(series, fir_weights, dft_matrix), samples)
    channel_id, slot_live = slot_lookup(channel_owner, N_INP * SLOTS, SLOTS)
    row_index = jnp.arange(INPUTS, dtype=jnp.int32)
    upper_mask = row_index[:, None] <= row_index[None, :]

    def compute(chosen):
        real_rows = lax.dynamic_index_in_dim(spectra, chosen, axis=2, keepdims=False)
        imag_rows = lax.dynamic_index_in_dim(spectra, chosen + CHANNELS, axis=2, keepdims=False)
        real_vis = jnp.dot(real_rows, real_rows.T, preferred_element_type=jnp.float32) + jnp.dot(imag_rows, imag_rows.T, preferred_element_type=jnp.float32)
        imag_vis = jnp.dot(imag_rows, real_rows.T, preferred_element_type=jnp.float32) - jnp.dot(real_rows, imag_rows.T, preferred_element_type=jnp.float32)
        packed = jnp.where(upper_mask, real_vis, imag_vis) / FRAMES
        return (packed.astype(jnp.bfloat16), jnp.diagonal(real_vis) / FRAMES)

    def nothing(chosen):
        return (jnp.zeros((INPUTS, INPUTS), jnp.bfloat16), jnp.zeros((INPUTS,), jnp.float32))

    def one_slot(slot_pair):
        chosen, live_count = slot_pair
        return lax.cond(live_count > 0, compute, nothing, chosen)
    visibility, auto_power = lax.map(one_slot, (channel_id, slot_live))
    return (visibility, auto_power)
```

```python
import math

import jax
import jax.numpy as jnp
import numpy as np
from jax import lax
from jax.experimental import pallas as pl
from jax.experimental.pallas import tpu as pltpu
from jax.sharding import PartitionSpec as P

POINTS = 2048
HALF = POINTS // 2
CHANNELS = 768
TAPS = 4
FRAMES = 128
INPUTS = 1024
OWNERS = 128
SECS = 4
DEVS = OWNERS * SECS
IN_DEV = 8
FR_DEV = 32
ROWS = IN_DEV * FR_DEV
GROUP = FR_DEV
MIB = 1 << 20
NT = (((1,), (1,)), ((), ()))


def dft_tables():
    points = np.arange(HALF, dtype=np.int64)
    tables = []
    for parity in range(2):
        channels = np.arange(parity, CHANNELS, 2, dtype=np.int64)
        angles = (channels[:, None] * points[None, :] % POINTS) * (2.0 * math.pi / POINTS)
        tables.append(np.concatenate([np.cos(angles), -np.sin(angles)], axis=0))
    return (np.stack(tables) / math.sqrt(POINTS)).astype(jnp.bfloat16)


def pick_kernel(owner_ref, pick_ref):
    owner = owner_ref[...]

    def channel_at(axis):
        place = lax.broadcasted_iota(jnp.int32, (CHANNELS, CHANNELS), axis)
        return jnp.where(place < CHANNELS // 2, 2 * place, 2 * place - (CHANNELS - 1))

    earlier = (channel_at(0) < channel_at(1)).astype(jnp.float32).astype(jnp.bfloat16)
    owners = lax.broadcasted_iota(jnp.int32, (OWNERS, CHANNELS), 0)
    named = (owners == owner).astype(jnp.float32)
    counts = jnp.dot(named.astype(jnp.bfloat16), earlier, preferred_element_type=jnp.float32)
    rank = jnp.sum(counts * named, axis=0, keepdims=True).astype(jnp.int32)
    target = ((rank >> 1) * OWNERS + owner) * 2 + (rank & 1)
    target = jnp.where(rank < 2 * SECS, target, -1)
    for side in range(2):
        place = 2 * lax.broadcasted_iota(jnp.int32, (DEVS, CHANNELS), 0) + side
        pick_ref[side] = (place == target).astype(jnp.float32).astype(jnp.bfloat16)


def spectra_kernel(x_ref, prev_ref, w_ref, pick_ref, tab_hbm, out_ref, ext, filt, spec, picked, rows, tab, sem):
    load = pltpu.make_async_copy(tab_hbm, tab, sem)
    load.start()
    ext[:, 5:8, :] = prev_ref[...].astype(jnp.float32)
    ext[:, 8:, :] = x_ref[...].astype(jnp.float32)
    width = 256
    for chunk in range(HALF // width):
        low = pl.ds(chunk * width, width)
        high = pl.ds(HALF + chunk * width, width)

        def fir(i, lanes):
            total = jnp.zeros((FR_DEV, width), jnp.float32)
            for tap in range(TAPS):
                total = total + w_ref[tap : tap + 1, lanes] * ext[i, 8 - tap : 8 - tap + FR_DEV, lanes]
            return total

        for i in range(IN_DEV):
            first, second = fir(i, low), fir(i, high)
            filt[0, i * FR_DEV : (i + 1) * FR_DEV, low] = (first + second).astype(jnp.bfloat16)
            filt[1, i * FR_DEV : (i + 1) * FR_DEV, low] = (first - second).astype(jnp.bfloat16)
    load.wait()
    part = CHANNELS // 2
    for parity in range(2):
        both = lax.dot_general(tab[parity], filt[parity], NT, preferred_element_type=jnp.float32)
        spec[0, parity * part : (parity + 1) * part, :] = both[:part].astype(jnp.bfloat16)
        spec[1, parity * part : (parity + 1) * part, :] = both[part:].astype(jnp.bfloat16)
    here = lax.axis_index("sec")
    for place in range(4):
        kind = (place - here) & 3
        picked[place] = jnp.dot(pick_ref[kind >> 1], spec[kind & 1], preferred_element_type=jnp.float32)
    step = 64
    group = lax.broadcasted_iota(jnp.int32, (step, 128), 1) // GROUP
    lower, even = group < 2, (group & 1) == 0
    for start in range(0, DEVS, step):
        for high in range(2):
            a = [picked[k, start : start + step, high * 128 : (high + 1) * 128] for k in range(4)]
            b0 = jnp.where(lower, a[0], pltpu.roll(a[2], 64, 1))
            b2 = jnp.where(lower, pltpu.roll(a[0], 64, 1), a[2])
            b1 = jnp.where(lower, a[1], pltpu.roll(a[3], 64, 1))
            b3 = jnp.where(lower, pltpu.roll(a[1], 64, 1), a[3])
            c = [
                jnp.where(even, b0, pltpu.roll(b1, 32, 1)),
                jnp.where(even, pltpu.roll(b0, 96, 1), b1),
                jnp.where(even, b2, pltpu.roll(b3, 32, 1)),
                jnp.where(even, pltpu.roll(b2, 96, 1), b3),
            ]
            for j in range(4):
                rows[pl.ds(start * IN_DEV + high * 4 + j, step, stride=IN_DEV), :] = c[j]
        span = slice(start * IN_DEV, (start + step) * IN_DEV)
        out_ref[span, :] = rows[span, :].astype(jnp.bfloat16)


def cross_kernel(r_ref, vis_hbm, auto_ref, plain, twist, out, sems):
    step = 128
    group = lax.broadcasted_iota(jnp.int32, (step, 128), 1) // GROUP
    tile = 256
    tiles = INPUTS // tile
    above = lax.broadcasted_iota(jnp.int32, (tile, tile), 0) <= lax.broadcasted_iota(jnp.int32, (tile, tile), 1)
    on_diag = lax.broadcasted_iota(jnp.int32, (tile, tile), 0) == lax.broadcasted_iota(jnp.int32, (tile, tile), 1)
    copies = []
    for slot in range(2):
        for start in range(0, INPUTS, step):
            span = slice(start, start + step)
            got = [r_ref[x, span, :].astype(jnp.float32) for x in range(SECS)]

            def part(kind):
                value = got[(0 - kind) % 4]
                for j in range(1, 4):
                    value = jnp.where(group == j, got[(j - kind) % 4], value)
                return value

            re = part(2 * slot)
            im = pltpu.roll(part(2 * slot + 1), 96, 1)
            plain[slot, span, :128] = re.astype(jnp.bfloat16)
            plain[slot, span, 128:] = im.astype(jnp.bfloat16)
            twist[slot, span, :128] = im.astype(jnp.bfloat16)
            twist[slot, span, 128:] = (-re).astype(jnp.bfloat16)
        for r in range(tiles):
            mine = slice(r * tile, (r + 1) * tile)
            for c in range(tiles):
                other = slice(c * tile, (c + 1) * tile)
                if c >= r:
                    real = lax.dot_general(
                        plain[slot, mine, :], plain[slot, other, :], NT, preferred_element_type=jnp.float32
                    ) * (1.0 / FRAMES)
                if c <= r:
                    imag = lax.dot_general(
                        twist[slot, mine, :], plain[slot, other, :], NT, preferred_element_type=jnp.float32
                    ) * (1.0 / FRAMES)
                if c == r:
                    value = jnp.where(above, real, imag)
                    auto_ref[slot : slot + 1, other] = jnp.sum(
                        jnp.where(on_diag, real, 0.0), axis=0, keepdims=True
                    )
                else:
                    value = real if c > r else imag
                out[slot, mine, other] = value.astype(jnp.bfloat16)
            copy = pltpu.make_async_copy(out.at[slot, mine], vis_hbm.at[slot, mine], sems.at[slot, r])
            copy.start()
            copies.append(copy)
    for copy in copies:
        copy.wait()


VMEM = pl.BlockSpec(memory_space=pltpu.VMEM)
ANY = pl.BlockSpec(memory_space=pl.ANY)


def local(samples, fir_weights, channel_owner):
    last_frames = samples[:, FR_DEV - (TAPS - 1) :, :]
    previous = lax.ppermute(last_frames, "sec", [(i, i + 1) for i in range(SECS - 1)])
    owner = channel_owner.reshape(CHANNELS // 2, 2).T.reshape(1, CHANNELS)
    pick = pl.pallas_call(
        pick_kernel,
        out_shape=jax.ShapeDtypeStruct((2, DEVS, CHANNELS), jnp.bfloat16),
        in_specs=[VMEM],
        out_specs=VMEM,
        compiler_params=pltpu.CompilerParams(vmem_limit_bytes=24 * MIB),
        cost_estimate=pl.CostEstimate(flops=2 * OWNERS * CHANNELS**2, bytes_accessed=4 * MIB, transcendentals=0),
        name="pick",
    )(owner)
    buffer = pl.pallas_call(
        spectra_kernel,
        out_shape=jax.ShapeDtypeStruct((DEVS * IN_DEV, 128), jnp.bfloat16),
        in_specs=[VMEM, VMEM, VMEM, VMEM, ANY],
        out_specs=VMEM,
        scratch_shapes=[
            pltpu.VMEM((IN_DEV, 8 + FR_DEV, POINTS), jnp.float32),
            pltpu.VMEM((2, ROWS, HALF), jnp.bfloat16),
            pltpu.VMEM((2, CHANNELS, ROWS), jnp.bfloat16),
            pltpu.VMEM((4, DEVS, ROWS), jnp.float32),
            pltpu.VMEM((DEVS * IN_DEV, 128), jnp.float32),
            pltpu.VMEM((2, CHANNELS, HALF), jnp.bfloat16),
            pltpu.SemaphoreType.DMA(()),
        ],
        compiler_params=pltpu.CompilerParams(vmem_limit_bytes=32 * MIB),
        cost_estimate=pl.CostEstimate(flops=4 * ROWS * HALF * CHANNELS, bytes_accessed=8 * MIB, transcendentals=0),
        name="spectra",
    )(samples, previous, fir_weights, pick, jnp.asarray(dft_tables()))
    received = lax.all_to_all(buffer, ("sec", "inp"), split_axis=0, concat_axis=0, tiled=True)
    visibility, auto_power = pl.pallas_call(
        cross_kernel,
        out_shape=(
            jax.ShapeDtypeStruct((2, INPUTS, INPUTS), jnp.bfloat16),
            jax.ShapeDtypeStruct((2, INPUTS), jnp.float32),
        ),
        in_specs=[VMEM],
        out_specs=(ANY, VMEM),
        scratch_shapes=[
            pltpu.VMEM((2, INPUTS, 256), jnp.bfloat16),
            pltpu.VMEM((2, INPUTS, 256), jnp.bfloat16),
            pltpu.VMEM((2, INPUTS, INPUTS), jnp.bfloat16),
            pltpu.SemaphoreType.DMA((2, 4)),
        ],
        compiler_params=pltpu.CompilerParams(vmem_limit_bytes=24 * MIB),
        name="cross",
    )(received.reshape(SECS, INPUTS, 128))
    return (visibility, auto_power)


def solution(mesh):
    in_specs = (P("inp", "sec", None), P(), P())
    out_specs = (P(("inp", "sec"), None, None), P(("inp", "sec"), None))
    return jax.shard_map(local, mesh=mesh, in_specs=in_specs, out_specs=out_specs, check_vma=False)
```

```python
import math

import jax
import jax.numpy as jnp
import numpy as np
from jax import lax
from jax.experimental import pallas as pl
from jax.experimental.pallas import tpu as pltpu
from jax.sharding import PartitionSpec as P

POINTS = 2048
HALF = POINTS // 2
CHANNELS = 768
PART = CHANNELS // 2
TAPS = 4
FRAMES = 128
INPUTS = 1024
OWNERS = 128
SECS = 4
DEVS = OWNERS * SECS
IN_DEV = 8
FR_DEV = 32
ROWS = IN_DEV * FR_DEV
EDGE = 8
WIDTH = 256
MIB = 1 << 20
NT = (((1,), (1,)), ((), ()))


def dft_tables():
    points = np.arange(HALF, dtype=np.int64)
    tables = []
    for parity in range(2):
        channels = np.arange(parity, CHANNELS, 2, dtype=np.int64)
        angles = (points[:, None] * channels[None, :] % POINTS) * (2.0 * math.pi / POINTS)
        tables.append(np.concatenate([np.cos(angles), -np.sin(angles)], axis=1))
    return (np.stack(tables) / math.sqrt(POINTS)).astype(jnp.bfloat16)


def as_bf16(mask):
    return mask.astype(jnp.float32).astype(jnp.bfloat16)


def pick_matrix(owner, pick_ref):
    def channel_at(axis):
        place = lax.broadcasted_iota(jnp.int32, (CHANNELS, CHANNELS), axis)
        return jnp.where(place < PART, 2 * place, 2 * place - (CHANNELS - 1))

    to_place = as_bf16(lax.broadcasted_iota(jnp.int32, (CHANNELS, CHANNELS), 0) == channel_at(1))
    spread = jnp.broadcast_to(owner.astype(jnp.float32), (8, CHANNELS)).astype(jnp.bfloat16)
    owner = jnp.dot(spread, to_place, preferred_element_type=jnp.float32)[:1].astype(jnp.int32)
    earlier = as_bf16(channel_at(0) < channel_at(1))
    named = (lax.broadcasted_iota(jnp.int32, (OWNERS, CHANNELS), 0) == owner).astype(jnp.float32)
    counts = jnp.dot(named.astype(jnp.bfloat16), earlier, preferred_element_type=jnp.float32)
    rank = jnp.sum(counts * named, axis=0, keepdims=True).astype(jnp.int32)
    target = ((rank >> 1) * OWNERS + owner) * 2 + (rank & 1)
    target = jnp.where(rank < 2 * SECS, target, -1)
    for side in range(2):
        place = 2 * lax.broadcasted_iota(jnp.int32, (DEVS, CHANNELS), 0) + side
        pick_ref[side] = as_bf16(place == target)


def head_kernel(owner_hbm, x_hbm, w_hbm, tab_hbm, pick_ref, filt_ref, edge_ref, tab_ref, owner, x, w, ext, sems):
    loads = [
        pltpu.make_async_copy(source, target, sems.at[i])
        for i, (source, target) in enumerate(((owner_hbm, owner), (x_hbm, x), (w_hbm, w), (tab_hbm, tab_ref)))
    ]
    for load in loads:
        load.start()
    loads[0].wait()
    pick_matrix(owner[...].reshape(1, CHANNELS), pick_ref)
    loads[1].wait()
    loads[2].wait()
    ext[:, :EDGE, :] = jnp.zeros((IN_DEV, EDGE, POINTS), jnp.float32)
    ext[:, EDGE:, :] = x[...].astype(jnp.float32)
    for chunk in range(HALF // WIDTH):
        low = pl.ds(chunk * WIDTH, WIDTH)
        high = pl.ds(HALF + chunk * WIDTH, WIDTH)

        def fir(i, lanes):
            total = w[0:1, lanes] * ext[i, EDGE : EDGE + FR_DEV, lanes]
            for tap in range(1, TAPS):
                total = total + w[tap : tap + 1, lanes] * ext[i, EDGE - tap : EDGE - tap + FR_DEV, lanes]
            return total

        for i in range(IN_DEV):
            first, second = fir(i, low), fir(i, high)
            edge_ref[i, :, low] = first[:EDGE]
            edge_ref[i, :, high] = second[:EDGE]
            filt_ref[0, i * FR_DEV : (i + 1) * FR_DEV, low] = (first + second).astype(jnp.bfloat16)
            filt_ref[1, i * FR_DEV : (i + 1) * FR_DEV, low] = (first - second).astype(jnp.bfloat16)
    loads[3].wait()


def spectra_kernel(prev_ref, w_ref, pick_ref, filt_ref, edge_ref, tab_ref, out_ref, ext, filt, spec, picked, rows):
    filt[...] = filt_ref[...]
    ext[:, :EDGE, :] = jnp.zeros((IN_DEV, EDGE, POINTS), jnp.float32)
    ext[:, EDGE:, :] = jnp.zeros((IN_DEV, EDGE, POINTS), jnp.float32)
    ext[:, EDGE - (TAPS - 1) : EDGE, :] = prev_ref[...].astype(jnp.float32)

    def fir(i, lanes):
        total = edge_ref[i, :, lanes]
        for tap in range(1, TAPS):
            total = total + w_ref[tap : tap + 1, lanes] * ext[i, EDGE - tap : 2 * EDGE - tap, lanes]
        return total

    for i in range(IN_DEV):
        first, second = fir(i, slice(0, HALF)), fir(i, slice(HALF, POINTS))
        filt[0, i * FR_DEV : i * FR_DEV + EDGE, :] = (first + second).astype(jnp.bfloat16)
        filt[1, i * FR_DEV : i * FR_DEV + EDGE, :] = (first - second).astype(jnp.bfloat16)
    for parity in range(2):
        both = jnp.dot(filt[parity], tab_ref[parity], preferred_element_type=jnp.float32).astype(jnp.bfloat16)
        columns = slice(parity * PART, (parity + 1) * PART)
        for i in range(IN_DEV):
            mine = both[i * FR_DEV : (i + 1) * FR_DEV]
            spec[2 * i * FR_DEV : (2 * i + 1) * FR_DEV, columns] = mine[:, :PART]
            spec[(2 * i + 1) * FR_DEV : (2 * i + 2) * FR_DEV, columns] = mine[:, PART:]
    flip = lax.axis_index("sec") & 1
    step = 64
    lower = lax.broadcasted_iota(jnp.int32, (step, 128), 1) < 64
    for quad in range(2):
        source = spec[quad * 256 : (quad + 1) * 256, :]
        for side in range(2):
            picked[quad, side] = lax.dot_general(pick_ref[side ^ flip], source, NT, preferred_element_type=jnp.float32)
        for start in range(0, DEVS, step):
            for pair in range(2):
                a, b = (picked[quad, side, start : start + step, pair * 128 : (pair + 1) * 128] for side in range(2))
                c = (jnp.where(lower, a, pltpu.roll(b, 64, 1)), jnp.where(lower, pltpu.roll(a, 64, 1), b))
                for j in range(2):
                    rows[pl.ds(start * IN_DEV + quad * 4 + pair * 2 + j, step, stride=IN_DEV), :] = c[j]
    out_ref[...] = rows[...].astype(jnp.bfloat16)


def cross_kernel(r_ref, vis_hbm, auto_ref, plain, twist, out, sems):
    tile = 256
    tiles = INPUTS // tile
    row = lax.broadcasted_iota(jnp.int32, (tile, tile), 0)
    column = lax.broadcasted_iota(jnp.int32, (tile, tile), 1)
    above, on_diag = row <= column, row == column
    turn = jnp.where(column == row - FR_DEV, 1.0, 0.0) * jnp.where((row // FR_DEV) % 2 == 1, 1.0, 0.0)
    turn = turn - jnp.where(column == row + FR_DEV, 1.0, 0.0) * jnp.where((row // FR_DEV) % 2 == 0, 1.0, 0.0)
    turn = turn.astype(jnp.bfloat16)
    lower = lax.broadcasted_iota(jnp.int32, (INPUTS, 128), 1) < 64
    copies = []
    for slot in range(2):
        for pair in range(2):
            first, second = r_ref[2 * pair + slot], r_ref[2 * pair + 1 - slot]
            plain[slot, :, pair * 128 : (pair + 1) * 128] = jnp.where(lower, first, second)
        twist[slot] = jnp.dot(plain[slot], turn, preferred_element_type=jnp.float32).astype(jnp.bfloat16)
        for r in range(tiles):
            mine = slice(r * tile, (r + 1) * tile)
            for c in range(tiles):
                other = slice(c * tile, (c + 1) * tile)
                if c >= r:
                    real = lax.dot_general(
                        plain[slot, mine, :], plain[slot, other, :], NT, preferred_element_type=jnp.float32
                    ) * (1.0 / FRAMES)
                if c <= r:
                    imag = lax.dot_general(
                        twist[slot, mine, :], plain[slot, other, :], NT, preferred_element_type=jnp.float32
                    ) * (1.0 / FRAMES)
                if c == r:
                    value = jnp.where(above, real, imag)
                    auto_ref[slot : slot + 1, other] = jnp.sum(
                        jnp.where(on_diag, real, 0.0), axis=0, keepdims=True
                    )
                else:
                    value = real if c > r else imag
                out[slot, mine, other] = value.astype(jnp.bfloat16)
            copy = pltpu.make_async_copy(out.at[slot, mine], vis_hbm.at[slot, mine], sems.at[slot, r])
            copy.start()
            copies.append(copy)
    for copy in copies:
        copy.wait()


VMEM = pl.BlockSpec(memory_space=pltpu.VMEM)
HBM = pl.BlockSpec(memory_space=pltpu.HBM)


def in_hbm(value):
    return pltpu.with_memory_space_constraint(value, pltpu.HBM)


def shaped(*shape, dtype=jnp.bfloat16):
    return jax.ShapeDtypeStruct(shape, dtype)


def local(samples, fir_weights, channel_owner):
    last_frames = samples[:, FR_DEV - (TAPS - 1) :, :]
    previous = lax.ppermute(last_frames, "sec", [(i, i + 1) for i in range(SECS - 1)])
    pick, filtered, edge, table = pl.pallas_call(
        head_kernel,
        out_shape=(
            shaped(2, DEVS, CHANNELS),
            shaped(2, ROWS, HALF),
            shaped(IN_DEV, EDGE, POINTS, dtype=jnp.float32),
            shaped(2, HALF, CHANNELS),
        ),
        in_specs=[HBM] * 4,
        out_specs=(VMEM,) * 4,
        scratch_shapes=[
            pltpu.VMEM((CHANNELS,), jnp.int32),
            pltpu.VMEM((IN_DEV, FR_DEV, POINTS), jnp.bfloat16),
            pltpu.VMEM((TAPS, POINTS), jnp.float32),
            pltpu.VMEM((IN_DEV, EDGE + FR_DEV, POINTS), jnp.float32),
            pltpu.SemaphoreType.DMA((4,)),
        ],
        compiler_params=pltpu.CompilerParams(vmem_limit_bytes=24 * MIB),
        cost_estimate=pl.CostEstimate(flops=2 * OWNERS * CHANNELS**2, bytes_accessed=8 * MIB, transcendentals=0),
        name="head",
    )(*(in_hbm(value) for value in (channel_owner, samples, fir_weights, jnp.asarray(dft_tables()))))
    buffer = pl.pallas_call(
        spectra_kernel,
        out_shape=shaped(DEVS * IN_DEV, 128),
        in_specs=[VMEM] * 6,
        out_specs=VMEM,
        scratch_shapes=[
            pltpu.VMEM((IN_DEV, 2 * EDGE, POINTS), jnp.float32),
            pltpu.VMEM((2, ROWS, HALF), jnp.bfloat16),
            pltpu.VMEM((2 * ROWS, CHANNELS), jnp.bfloat16),
            pltpu.VMEM((2, 2, DEVS, 256), jnp.float32),
            pltpu.VMEM((DEVS * IN_DEV, 128), jnp.float32),
        ],
        compiler_params=pltpu.CompilerParams(vmem_limit_bytes=32 * MIB),
        cost_estimate=pl.CostEstimate(flops=4 * ROWS * HALF * CHANNELS, bytes_accessed=8 * MIB, transcendentals=0),
        name="spectra",
    )(previous, fir_weights, pick, filtered, edge, table)
    received = lax.all_to_all(buffer, ("sec", "inp"), split_axis=0, concat_axis=0, tiled=True)
    visibility, auto_power = pl.pallas_call(
        cross_kernel,
        out_shape=(shaped(2, INPUTS, INPUTS), shaped(2, INPUTS, dtype=jnp.float32)),
        in_specs=[VMEM],
        out_specs=(HBM, VMEM),
        scratch_shapes=[
            pltpu.VMEM((2, INPUTS, 256), jnp.bfloat16),
            pltpu.VMEM((2, INPUTS, 256), jnp.bfloat16),
            pltpu.VMEM((2, INPUTS, INPUTS), jnp.bfloat16),
            pltpu.SemaphoreType.DMA((2, 4)),
        ],
        compiler_params=pltpu.CompilerParams(vmem_limit_bytes=24 * MIB),
        name="cross",
    )(received.reshape(SECS, INPUTS, 128))
    return (visibility, auto_power)


def solution(mesh):
    in_specs = (P("inp", "sec", None), P(), P())
    out_specs = (P(("inp", "sec"), None, None), P(("inp", "sec"), None))
    return jax.shard_map(local, mesh=mesh, in_specs=in_specs, out_specs=out_specs, check_vma=False)
```

```python
import math

import jax
import jax.numpy as jnp
import numpy as np
from jax import lax
from jax.experimental import pallas as pl
from jax.experimental.pallas import tpu as pltpu
from jax.sharding import PartitionSpec as P

POINTS = 2048
HALF = POINTS // 2
CHANNELS = 768
PART = CHANNELS // 2
TAPS = 4
FRAMES = 128
INPUTS = 1024
OWNERS = 128
SECS = 4
DEVS = OWNERS * SECS
IN_DEV = 8
FR_DEV = 32
ROWS = IN_DEV * FR_DEV
EDGE = 8
WIDTH = 256
MIB = 1 << 20
NT = (((1,), (1,)), ((), ()))


def dft_tables():
    points = np.arange(HALF, dtype=np.int64)
    tables = []
    for parity in range(2):
        channels = np.arange(parity, CHANNELS, 2, dtype=np.int64)
        angles = (points[:, None] * channels[None, :] % POINTS) * (2.0 * math.pi / POINTS)
        tables.append(np.concatenate([np.cos(angles), -np.sin(angles)], axis=1))
    return (np.stack(tables) / math.sqrt(POINTS)).astype(jnp.bfloat16)


def as_bf16(mask):
    return mask.astype(jnp.float32).astype(jnp.bfloat16)


def channel_at(axis):
    place = lax.broadcasted_iota(jnp.int32, (CHANNELS, CHANNELS), axis)
    return jnp.where(place < PART, 2 * place, 2 * place - (CHANNELS - 1))


def pick_matrix(owner, to_place, earlier, pick_ref):
    spread = jnp.broadcast_to(owner.astype(jnp.float32), (8, CHANNELS)).astype(jnp.bfloat16)
    owner = jnp.dot(spread, to_place, preferred_element_type=jnp.float32)[:1].astype(jnp.int32)
    named = (lax.broadcasted_iota(jnp.int32, (OWNERS, CHANNELS), 0) == owner).astype(jnp.float32)
    counts = jnp.dot(named.astype(jnp.bfloat16), earlier, preferred_element_type=jnp.float32)
    rank = jnp.sum(counts * named, axis=0, keepdims=True).astype(jnp.int32)
    target = ((rank >> 1) * OWNERS + owner) * 2 + (rank & 1)
    target = jnp.where(rank < 2 * SECS, target, -1)
    for side in range(2):
        place = 2 * lax.broadcasted_iota(jnp.int32, (DEVS, CHANNELS), 0) + side
        pick_ref[side] = as_bf16(place == target)


def transform(rows, frames, table, parity, spec_ref):
    both = jnp.dot(rows, table, preferred_element_type=jnp.float32).astype(jnp.bfloat16)
    columns = slice(parity * PART, (parity + 1) * PART)
    for i in range(IN_DEV):
        mine = both[i * frames : (i + 1) * frames]
        spec_ref[2 * i * FR_DEV : 2 * i * FR_DEV + frames, columns] = mine[:, :PART]
        spec_ref[(2 * i + 1) * FR_DEV : (2 * i + 1) * FR_DEV + frames, columns] = mine[:, PART:]


def head_kernel(
    owner_hbm, x_hbm, w_hbm, tab_hbm, pick_ref, spec_ref, edge_ref, tab_ref, owner, x, w, filt, to_place, earlier, sems
):
    pairs = ((owner_hbm, owner), (x_hbm, x), (w_hbm, w), (tab_hbm.at[0], tab_ref.at[0]), (tab_hbm.at[1], tab_ref.at[1]))
    loads = [pltpu.make_async_copy(source, target, sems.at[i]) for i, (source, target) in enumerate(pairs)]
    for load in loads:
        load.start()
    to_place[...] = as_bf16(lax.broadcasted_iota(jnp.int32, (CHANNELS, CHANNELS), 0) == channel_at(1))
    earlier[...] = as_bf16(channel_at(0) < channel_at(1))
    loads[0].wait()
    pick_matrix(owner[...].reshape(1, CHANNELS), to_place[...], earlier[...], pick_ref)
    loads[1].wait()
    loads[2].wait()
    frame = lax.broadcasted_iota(jnp.int32, (FR_DEV, WIDTH), 0)

    def fir(i, lanes):
        now = x[i, :, lanes].astype(jnp.float32)
        total = w[0:1, lanes] * now
        for tap in range(1, TAPS):
            total = total + w[tap : tap + 1, lanes] * jnp.where(frame >= tap, pltpu.roll(now, tap, 0), 0.0)
        return total

    for chunk in range(HALF // WIDTH):
        low = pl.ds(chunk * WIDTH, WIDTH)
        high = pl.ds(HALF + chunk * WIDTH, WIDTH)
        for i in range(IN_DEV):
            first, second = fir(i, low), fir(i, high)
            edge_ref[i, :, low] = first[:EDGE]
            edge_ref[i, :, high] = second[:EDGE]
            filt[0, i * FR_DEV : (i + 1) * FR_DEV, low] = (first + second).astype(jnp.bfloat16)
            filt[1, i * FR_DEV : (i + 1) * FR_DEV, low] = (first - second).astype(jnp.bfloat16)
    for parity in range(2):
        loads[3 + parity].wait()
        transform(filt[parity], FR_DEV, tab_ref[parity], parity, spec_ref)


def spectra_kernel(prev_ref, w_ref, pick_ref, spec_in, edge_ref, tab_ref, out_ref, spec_ref, ext, filt, picked, rows):
    spec_ref[...] = spec_in[...]
    ext[:, :EDGE, :] = jnp.zeros((IN_DEV, EDGE, POINTS), jnp.float32)
    ext[:, EDGE:, :] = jnp.zeros((IN_DEV, EDGE, POINTS), jnp.float32)
    ext[:, EDGE - (TAPS - 1) : EDGE, :] = prev_ref[...].astype(jnp.float32)

    def fir(i, lanes):
        total = edge_ref[i, :, lanes]
        for tap in range(1, TAPS):
            total = total + w_ref[tap : tap + 1, lanes] * ext[i, EDGE - tap : 2 * EDGE - tap, lanes]
        return total

    for i in range(IN_DEV):
        first, second = fir(i, slice(0, HALF)), fir(i, slice(HALF, POINTS))
        filt[0, i * EDGE : (i + 1) * EDGE, :] = (first + second).astype(jnp.bfloat16)
        filt[1, i * EDGE : (i + 1) * EDGE, :] = (first - second).astype(jnp.bfloat16)
    for parity in range(2):
        transform(filt[parity], EDGE, tab_ref[parity], parity, spec_ref)
    flip = lax.axis_index("sec") & 1
    step = 64
    lower = lax.broadcasted_iota(jnp.int32, (step, 128), 1) < 64
    for quad in range(2):
        source = spec_ref[quad * 256 : (quad + 1) * 256, :]
        for side in range(2):
            picked[quad, side] = lax.dot_general(pick_ref[side ^ flip], source, NT, preferred_element_type=jnp.float32)
        for start in range(0, DEVS, step):
            for pair in range(2):
                a, b = (picked[quad, side, start : start + step, pair * 128 : (pair + 1) * 128] for side in range(2))
                c = (jnp.where(lower, a, pltpu.roll(b, 64, 1)), jnp.where(lower, pltpu.roll(a, 64, 1), b))
                for j in range(2):
                    rows[pl.ds(start * IN_DEV + quad * 4 + pair * 2 + j, step, stride=IN_DEV), :] = c[j]
    out_ref[...] = rows[...].astype(jnp.bfloat16)


def cross_kernel(r_ref, vis_hbm, auto_hbm, plain, twist, out, auto, sems, auto_sem):
    tile, half = 256, 128
    row = lax.broadcasted_iota(jnp.int32, (tile, tile), 0)
    column = lax.broadcasted_iota(jnp.int32, (tile, tile), 1)
    odd = (row // FR_DEV) % 2
    turn = jnp.where(column - row == FR_DEV * (1 - 2 * odd), (2 * odd - 1).astype(jnp.float32), 0.0)
    turn = turn.astype(jnp.bfloat16)
    small_row = lax.broadcasted_iota(jnp.int32, (half, half), 0)
    small_column = lax.broadcasted_iota(jnp.int32, (half, half), 1)
    above, on_diag = small_row <= small_column, small_row == small_column
    lower = lax.broadcasted_iota(jnp.int32, (INPUTS, 128), 1) < 64

    def prepare(slot):
        for pair in range(2):
            first, second = r_ref[2 * pair + slot], r_ref[2 * pair + 1 - slot]
            plain[slot, :, pair * 128 : (pair + 1) * 128] = jnp.where(lower, first, second)
        twist[slot] = jnp.dot(plain[slot], turn, preferred_element_type=jnp.float32).astype(jnp.bfloat16)

    copies = []
    prepare(0)
    for slot in range(2):
        for start in range(0, INPUTS, tile):
            end = start + tile
            mine = slice(start, end)
            real = lax.dot_general(
                plain[slot, mine, :], plain[slot, start:, :], NT, preferred_element_type=jnp.float32
            ) * (1.0 / FRAMES)
            imag = lax.dot_general(
                twist[slot, mine, :], plain[slot, :end, :], NT, preferred_element_type=jnp.float32
            ) * (1.0 / FRAMES)
            if start > 0:
                out[slot, mine, :start] = imag[:, :start].astype(jnp.bfloat16)
            if end < INPUTS:
                out[slot, mine, end:] = real[:, tile:].astype(jnp.bfloat16)
            middle = start + half
            out[slot, start:middle, middle:end] = real[:half, half:tile].astype(jnp.bfloat16)
            out[slot, middle:end, start:middle] = imag[half:, start:middle].astype(jnp.bfloat16)
            for part in range(2):
                here = slice(start + part * half, start + (part + 1) * half)
                inner = slice(part * half, (part + 1) * half)
                block = real[inner, inner]
                out[slot, here, here] = jnp.where(above, block, imag[inner, here]).astype(jnp.bfloat16)
                auto[slot : slot + 1, here] = jnp.sum(jnp.where(on_diag, block, 0.0), axis=0, keepdims=True)
            copy = pltpu.make_async_copy(out.at[slot, mine], vis_hbm.at[slot, mine], sems.at[slot, start // tile])
            copy.start()
            copies.append(copy)
            if slot == 0 and start == 0:
                prepare(1)
    copy = pltpu.make_async_copy(auto, auto_hbm, auto_sem)
    copy.start()
    copies.append(copy)
    for copy in copies:
        copy.wait()


VMEM = pl.BlockSpec(memory_space=pltpu.VMEM)
HBM = pl.BlockSpec(memory_space=pltpu.HBM)


def in_hbm(value):
    return pltpu.with_memory_space_constraint(value, pltpu.HBM)


def shaped(*shape, dtype=jnp.bfloat16):
    return jax.ShapeDtypeStruct(shape, dtype)


def local(samples, fir_weights, channel_owner):
    last_frames = samples[:, FR_DEV - (TAPS - 1) :, :]
    previous = lax.ppermute(last_frames, "sec", [(i, i + 1) for i in range(SECS - 1)])
    pick, partial, edge, table = pl.pallas_call(
        head_kernel,
        out_shape=(
            shaped(2, DEVS, CHANNELS),
            shaped(2 * ROWS, CHANNELS),
            shaped(IN_DEV, EDGE, POINTS, dtype=jnp.float32),
            shaped(2, HALF, CHANNELS),
        ),
        in_specs=[HBM] * 4,
        out_specs=(VMEM,) * 4,
        scratch_shapes=[
            pltpu.VMEM((CHANNELS,), jnp.int32),
            pltpu.VMEM((IN_DEV, FR_DEV, POINTS), jnp.bfloat16),
            pltpu.VMEM((TAPS, POINTS), jnp.float32),
            pltpu.VMEM((2, ROWS, HALF), jnp.bfloat16),
            pltpu.VMEM((CHANNELS, CHANNELS), jnp.bfloat16),
            pltpu.VMEM((CHANNELS, CHANNELS), jnp.bfloat16),
            pltpu.SemaphoreType.DMA((5,)),
        ],
        compiler_params=pltpu.CompilerParams(vmem_limit_bytes=24 * MIB),
        cost_estimate=pl.CostEstimate(flops=2 * OWNERS * CHANNELS**2, bytes_accessed=8 * MIB, transcendentals=0),
        name="head",
    )(*(in_hbm(value) for value in (channel_owner, samples, fir_weights, jnp.asarray(dft_tables()))))
    buffer = pl.pallas_call(
        spectra_kernel,
        out_shape=shaped(DEVS * IN_DEV, 128),
        in_specs=[VMEM] * 6,
        out_specs=VMEM,
        scratch_shapes=[
            pltpu.VMEM((2 * ROWS, CHANNELS), jnp.bfloat16),
            pltpu.VMEM((IN_DEV, 2 * EDGE, POINTS), jnp.float32),
            pltpu.VMEM((2, IN_DEV * EDGE, HALF), jnp.bfloat16),
            pltpu.VMEM((2, 2, DEVS, 256), jnp.float32),
            pltpu.VMEM((DEVS * IN_DEV, 128), jnp.float32),
        ],
        compiler_params=pltpu.CompilerParams(vmem_limit_bytes=32 * MIB),
        cost_estimate=pl.CostEstimate(flops=4 * ROWS * HALF * CHANNELS, bytes_accessed=8 * MIB, transcendentals=0),
        name="spectra",
    )(previous, fir_weights, pick, partial, edge, table)
    received = lax.all_to_all(buffer, ("sec", "inp"), split_axis=0, concat_axis=0, tiled=True)
    visibility, auto_power = pl.pallas_call(
        cross_kernel,
        out_shape=(shaped(2, INPUTS, INPUTS), shaped(2, INPUTS, dtype=jnp.float32)),
        in_specs=[VMEM],
        out_specs=(HBM, HBM),
        scratch_shapes=[
            pltpu.VMEM((2, INPUTS, 256), jnp.bfloat16),
            pltpu.VMEM((2, INPUTS, 256), jnp.bfloat16),
            pltpu.VMEM((2, INPUTS, INPUTS), jnp.bfloat16),
            pltpu.VMEM((2, INPUTS), jnp.float32),
            pltpu.SemaphoreType.DMA((2, 4)),
            pltpu.SemaphoreType.DMA(()),
        ],
        compiler_params=pltpu.CompilerParams(vmem_limit_bytes=24 * MIB),
        name="cross",
    )(received.reshape(SECS, INPUTS, 128))
    return (visibility, auto_power)


def solution(mesh):
    in_specs = (P("inp", "sec", None), P(), P())
    out_specs = (P(("inp", "sec"), None, None), P(("inp", "sec"), None))
    return jax.shard_map(local, mesh=mesh, in_specs=in_specs, out_specs=out_specs, check_vma=False)
```

```python
import math

import jax
import jax.numpy as jnp
import numpy as np
from jax import lax
from jax.experimental import pallas as pl
from jax.experimental.pallas import tpu as pltpu
from jax.sharding import PartitionSpec as P

POINTS = 2048
HALF = POINTS // 2
CHANNELS = 768
PART = CHANNELS // 2
TAPS = 4
FRAMES = 128
INPUTS = 1024
OWNERS = 128
SECS = 4
DEVS = OWNERS * SECS
IN_DEV = 8
FR_DEV = 32
ROWS = IN_DEV * FR_DEV
EDGE = 8
WIDTH = 256
MIB = 1 << 20
NT = (((1,), (1,)), ((), ()))


def dft_tables():
    points = np.arange(HALF, dtype=np.int64)
    tables = []
    for parity in range(2):
        channels = np.arange(parity, CHANNELS, 2, dtype=np.int64)
        angles = (points[:, None] * channels[None, :] % POINTS) * (2.0 * math.pi / POINTS)
        tables.append(np.concatenate([np.cos(angles), -np.sin(angles)], axis=1))
    return (np.stack(tables) / math.sqrt(POINTS)).astype(jnp.bfloat16)


def as_bf16(mask):
    return mask.astype(jnp.float32).astype(jnp.bfloat16)


def channel_at(axis):
    place = lax.broadcasted_iota(jnp.int32, (CHANNELS, CHANNELS), axis)
    return jnp.where(place < PART, 2 * place, 2 * place - (CHANNELS - 1))


def pick_matrix(owner, to_place, earlier, pick_ref):
    spread = jnp.broadcast_to(owner.astype(jnp.float32), (8, CHANNELS)).astype(jnp.bfloat16)
    owner = jnp.dot(spread, to_place, preferred_element_type=jnp.float32)[:1].astype(jnp.int32)
    named = (lax.broadcasted_iota(jnp.int32, (OWNERS, CHANNELS), 0) == owner).astype(jnp.float32)
    counts = jnp.dot(named.astype(jnp.bfloat16), earlier, preferred_element_type=jnp.float32)
    rank = jnp.sum(counts * named, axis=0, keepdims=True).astype(jnp.int32)
    target = ((rank >> 1) * OWNERS + owner) * 2 + (rank & 1)
    target = jnp.where(rank < 2 * SECS, target, -1)
    for side in range(2):
        place = 2 * lax.broadcasted_iota(jnp.int32, (DEVS, CHANNELS), 0) + side
        pick_ref[side] = as_bf16(place == target)


def head_kernel(
    owner_hbm, x_hbm, w_hbm, tab_hbm, pick_ref, filt_ref, edge_ref, tab_ref, owner, x, w, to_place, earlier, sems
):
    pairs = ((owner_hbm, owner), (x_hbm, x), (w_hbm, w), (tab_hbm, tab_ref))
    loads = [pltpu.make_async_copy(source, target, sems.at[i]) for i, (source, target) in enumerate(pairs)]
    for load in loads:
        load.start()
    to_place[...] = as_bf16(lax.broadcasted_iota(jnp.int32, (CHANNELS, CHANNELS), 0) == channel_at(1))
    earlier[...] = as_bf16(channel_at(0) < channel_at(1))
    loads[0].wait()
    pick_matrix(owner[...].reshape(1, CHANNELS), to_place[...], earlier[...], pick_ref)
    loads[1].wait()
    loads[2].wait()
    frame = lax.broadcasted_iota(jnp.int32, (FR_DEV, WIDTH), 0)

    def fir(i, lanes):
        now = x[i, :, lanes].astype(jnp.float32)
        total = w[0:1, lanes] * now
        for tap in range(1, TAPS):
            total = total + w[tap : tap + 1, lanes] * jnp.where(frame >= tap, pltpu.roll(now, tap, 0), 0.0)
        return total

    for chunk in range(HALF // WIDTH):
        low = pl.ds(chunk * WIDTH, WIDTH)
        high = pl.ds(HALF + chunk * WIDTH, WIDTH)
        for i in range(IN_DEV):
            first, second = fir(i, low), fir(i, high)
            edge_ref[i, :, low] = first[:EDGE]
            edge_ref[i, :, high] = second[:EDGE]
            filt_ref[0, i * FR_DEV : (i + 1) * FR_DEV, low] = (first + second).astype(jnp.bfloat16)
            filt_ref[1, i * FR_DEV : (i + 1) * FR_DEV, low] = (first - second).astype(jnp.bfloat16)
    loads[3].wait()


def spectra_kernel(prev_ref, w_ref, pick_ref, filt_ref, edge_ref, tab_ref, out_ref, ext, filt, spec, picked, rows):
    ext[:, :EDGE, :] = jnp.zeros((IN_DEV, EDGE, POINTS), jnp.float32)
    ext[:, EDGE:, :] = jnp.zeros((IN_DEV, EDGE, POINTS), jnp.float32)
    ext[:, EDGE - (TAPS - 1) : EDGE, :] = prev_ref[...].astype(jnp.float32)

    def fir(i, lanes):
        total = edge_ref[i, :, lanes]
        for tap in range(1, TAPS):
            total = total + w_ref[tap : tap + 1, lanes] * ext[i, EDGE - tap : 2 * EDGE - tap, lanes]
        return total

    for parity in range(2):
        filt[parity] = filt_ref[parity]
        for i in range(IN_DEV):
            first, second = fir(i, slice(0, HALF)), fir(i, slice(HALF, POINTS))
            both = first + second if parity == 0 else first - second
            filt[parity, i * FR_DEV : i * FR_DEV + EDGE, :] = both.astype(jnp.bfloat16)
        both = jnp.dot(filt[parity], tab_ref[parity], preferred_element_type=jnp.float32).astype(jnp.bfloat16)
        columns = slice(parity * PART, (parity + 1) * PART)
        for i in range(IN_DEV):
            mine = both[i * FR_DEV : (i + 1) * FR_DEV]
            spec[2 * i * FR_DEV : (2 * i + 1) * FR_DEV, columns] = mine[:, :PART]
            spec[(2 * i + 1) * FR_DEV : (2 * i + 2) * FR_DEV, columns] = mine[:, PART:]
    flip = lax.axis_index("sec") & 1
    step = 64
    lower = lax.broadcasted_iota(jnp.int32, (step, 128), 1) < 64
    for quad in range(2):
        source = spec[quad * 256 : (quad + 1) * 256, :]
        for side in range(2):
            picked[quad, side] = lax.dot_general(pick_ref[side ^ flip], source, NT, preferred_element_type=jnp.float32)
        for start in range(0, DEVS, step):
            for pair in range(2):
                a, b = (picked[quad, side, start : start + step, pair * 128 : (pair + 1) * 128] for side in range(2))
                c = (jnp.where(lower, a, pltpu.roll(b, 64, 1)), jnp.where(lower, pltpu.roll(a, 64, 1), b))
                for j in range(2):
                    rows[pl.ds(start * IN_DEV + quad * 4 + pair * 2 + j, step, stride=IN_DEV), :] = c[j]
    out_ref[...] = rows[...].astype(jnp.bfloat16)


def cross_kernel(r_ref, vis_hbm, auto_hbm, plain, twist, out, auto, sems, auto_sem):
    tile, half = 256, 128
    row = lax.broadcasted_iota(jnp.int32, (tile, tile), 0)
    column = lax.broadcasted_iota(jnp.int32, (tile, tile), 1)
    odd = (row // FR_DEV) % 2
    turn = jnp.where(column - row == FR_DEV * (1 - 2 * odd), (2 * odd - 1).astype(jnp.float32), 0.0)
    turn = turn.astype(jnp.bfloat16)
    small_row = lax.broadcasted_iota(jnp.int32, (half, half), 0)
    small_column = lax.broadcasted_iota(jnp.int32, (half, half), 1)
    above, on_diag = small_row <= small_column, small_row == small_column
    lower = lax.broadcasted_iota(jnp.int32, (INPUTS, 128), 1) < 64

    def prepare(slot):
        for pair in range(2):
            first, second = r_ref[2 * pair + slot], r_ref[2 * pair + 1 - slot]
            plain[slot, :, pair * 128 : (pair + 1) * 128] = jnp.where(lower, first, second)
        twist[slot] = jnp.dot(plain[slot], turn, preferred_element_type=jnp.float32).astype(jnp.bfloat16)

    copies = []
    prepare(0)
    for slot in range(2):
        for start in range(0, INPUTS, tile):
            end = start + tile
            mine = slice(start, end)
            real = lax.dot_general(
                plain[slot, mine, :], plain[slot, start:, :], NT, preferred_element_type=jnp.float32
            ) * (1.0 / FRAMES)
            imag = lax.dot_general(
                twist[slot, mine, :], plain[slot, :end, :], NT, preferred_element_type=jnp.float32
            ) * (1.0 / FRAMES)
            if start > 0:
                out[slot, mine, :start] = imag[:, :start].astype(jnp.bfloat16)
            if end < INPUTS:
                out[slot, mine, end:] = real[:, tile:].astype(jnp.bfloat16)
            middle = start + half
            out[slot, start:middle, middle:end] = real[:half, half:tile].astype(jnp.bfloat16)
            out[slot, middle:end, start:middle] = imag[half:, start:middle].astype(jnp.bfloat16)
            for part in range(2):
                here = slice(start + part * half, start + (part + 1) * half)
                inner = slice(part * half, (part + 1) * half)
                block = real[inner, inner]
                out[slot, here, here] = jnp.where(above, block, imag[inner, here]).astype(jnp.bfloat16)
                auto[slot : slot + 1, here] = jnp.sum(jnp.where(on_diag, block, 0.0), axis=0, keepdims=True)
            copy = pltpu.make_async_copy(out.at[slot, mine], vis_hbm.at[slot, mine], sems.at[slot, start // tile])
            copy.start()
            copies.append(copy)
            if slot == 0 and start == 0:
                prepare(1)
    copy = pltpu.make_async_copy(auto, auto_hbm, auto_sem)
    copy.start()
    copies.append(copy)
    for copy in copies:
        copy.wait()


VMEM = pl.BlockSpec(memory_space=pltpu.VMEM)
HBM = pl.BlockSpec(memory_space=pltpu.HBM)


def in_hbm(value):
    return pltpu.with_memory_space_constraint(value, pltpu.HBM)


def shaped(*shape, dtype=jnp.bfloat16):
    return jax.ShapeDtypeStruct(shape, dtype)


def local(samples, fir_weights, channel_owner):
    last_frames = samples[:, FR_DEV - (TAPS - 1) :, :]
    previous = lax.ppermute(last_frames, "sec", [(i, i + 1) for i in range(SECS - 1)])
    pick, filtered, edge, table = pl.pallas_call(
        head_kernel,
        out_shape=(
            shaped(2, DEVS, CHANNELS),
            shaped(2, ROWS, HALF),
            shaped(IN_DEV, EDGE, POINTS, dtype=jnp.float32),
            shaped(2, HALF, CHANNELS),
        ),
        in_specs=[HBM] * 4,
        out_specs=(VMEM,) * 4,
        scratch_shapes=[
            pltpu.VMEM((CHANNELS,), jnp.int32),
            pltpu.VMEM((IN_DEV, FR_DEV, POINTS), jnp.bfloat16),
            pltpu.VMEM((TAPS, POINTS), jnp.float32),
            pltpu.VMEM((CHANNELS, CHANNELS), jnp.bfloat16),
            pltpu.VMEM((CHANNELS, CHANNELS), jnp.bfloat16),
            pltpu.SemaphoreType.DMA((4,)),
        ],
        compiler_params=pltpu.CompilerParams(vmem_limit_bytes=24 * MIB),
        cost_estimate=pl.CostEstimate(flops=2 * OWNERS * CHANNELS**2, bytes_accessed=8 * MIB, transcendentals=0),
        name="head",
    )(*(in_hbm(value) for value in (channel_owner, samples, fir_weights, jnp.asarray(dft_tables()))))
    buffer = pl.pallas_call(
        spectra_kernel,
        out_shape=shaped(DEVS * IN_DEV, 128),
        in_specs=[VMEM] * 6,
        out_specs=VMEM,
        scratch_shapes=[
            pltpu.VMEM((IN_DEV, 2 * EDGE, POINTS), jnp.float32),
            pltpu.VMEM((2, ROWS, HALF), jnp.bfloat16),
            pltpu.VMEM((2 * ROWS, CHANNELS), jnp.bfloat16),
            pltpu.VMEM((2, 2, DEVS, 256), jnp.float32),
            pltpu.VMEM((DEVS * IN_DEV, 128), jnp.float32),
        ],
        compiler_params=pltpu.CompilerParams(vmem_limit_bytes=32 * MIB),
        cost_estimate=pl.CostEstimate(flops=4 * ROWS * HALF * CHANNELS, bytes_accessed=8 * MIB, transcendentals=0),
        name="spectra",
    )(previous, fir_weights, pick, filtered, edge, table)
    received = lax.all_to_all(buffer, ("sec", "inp"), split_axis=0, concat_axis=0, tiled=True)
    visibility, auto_power = pl.pallas_call(
        cross_kernel,
        out_shape=(shaped(2, INPUTS, INPUTS), shaped(2, INPUTS, dtype=jnp.float32)),
        in_specs=[VMEM],
        out_specs=(HBM, HBM),
        scratch_shapes=[
            pltpu.VMEM((2, INPUTS, 256), jnp.bfloat16),
            pltpu.VMEM((2, INPUTS, 256), jnp.bfloat16),
            pltpu.VMEM((2, INPUTS, INPUTS), jnp.bfloat16),
            pltpu.VMEM((2, INPUTS), jnp.float32),
            pltpu.SemaphoreType.DMA((2, 4)),
            pltpu.SemaphoreType.DMA(()),
        ],
        compiler_params=pltpu.CompilerParams(vmem_limit_bytes=24 * MIB),
        name="cross",
    )(received.reshape(SECS, INPUTS, 128))
    return (visibility, auto_power)


def solution(mesh):
    in_specs = (P("inp", "sec", None), P(), P())
    out_specs = (P(("inp", "sec"), None, None), P(("inp", "sec"), None))
    return jax.shard_map(local, mesh=mesh, in_specs=in_specs, out_specs=out_specs, check_vma=False)
```

```python
import math

import jax
import jax.numpy as jnp
import numpy as np
from jax import lax
from jax.experimental import pallas as pl
from jax.experimental.pallas import tpu as pltpu
from jax.sharding import PartitionSpec as P

POINTS = 2048
HALF = POINTS // 2
CHANNELS = 768
PART = CHANNELS // 2
TAPS = 4
FRAMES = 128
INPUTS = 1024
OWNERS = 128
SECS = 4
DEVS = OWNERS * SECS
IN_DEV = 8
FR_DEV = 32
ROWS = IN_DEV * FR_DEV
EDGE = 8
WIDTH = 256
MIB = 1 << 20
NT = (((1,), (1,)), ((), ()))


def dft_tables():
    points = np.arange(HALF, dtype=np.int64)
    tables = []
    for parity in range(2):
        channels = np.arange(parity, CHANNELS, 2, dtype=np.int64)
        angles = (points[:, None] * channels[None, :] % POINTS) * (2.0 * math.pi / POINTS)
        tables.append(np.concatenate([np.cos(angles), -np.sin(angles)], axis=1))
    return (np.stack(tables) / math.sqrt(POINTS)).astype(jnp.bfloat16)


def as_bf16(mask):
    return mask.astype(jnp.float32).astype(jnp.bfloat16)


def channel_at(axis):
    place = lax.broadcasted_iota(jnp.int32, (CHANNELS, CHANNELS), axis)
    return jnp.where(place < PART, 2 * place, 2 * place - (CHANNELS - 1))


def pick_matrix(owner, to_place, earlier, pick_ref):
    spread = jnp.broadcast_to(owner.astype(jnp.float32), (8, CHANNELS)).astype(jnp.bfloat16)
    owner = jnp.dot(spread, to_place, preferred_element_type=jnp.float32)[:1].astype(jnp.int32)
    named = (lax.broadcasted_iota(jnp.int32, (OWNERS, CHANNELS), 0) == owner).astype(jnp.float32)
    counts = jnp.dot(named.astype(jnp.bfloat16), earlier, preferred_element_type=jnp.float32)
    rank = jnp.sum(counts * named, axis=0, keepdims=True).astype(jnp.int32)
    target = ((rank >> 1) * OWNERS + owner) * 2 + (rank & 1)
    target = jnp.where(rank < 2 * SECS, target, -1)
    for side in range(2):
        place = 2 * lax.broadcasted_iota(jnp.int32, (DEVS, CHANNELS), 0) + side
        pick_ref[side] = as_bf16(place == target)


def head_kernel(
    owner_hbm, x_hbm, w_hbm, tab_hbm, pick_ref, filt_ref, edge_ref, tab_ref, owner, x, w, to_place, earlier, sems
):
    pairs = ((owner_hbm, owner), (x_hbm, x), (w_hbm, w), (tab_hbm, tab_ref))
    loads = [pltpu.make_async_copy(source, target, sems.at[i]) for i, (source, target) in enumerate(pairs)]
    for load in loads:
        load.start()
    to_place[...] = as_bf16(lax.broadcasted_iota(jnp.int32, (CHANNELS, CHANNELS), 0) == channel_at(1))
    earlier[...] = as_bf16(channel_at(0) < channel_at(1))
    loads[0].wait()
    pick_matrix(owner[...].reshape(1, CHANNELS), to_place[...], earlier[...], pick_ref)
    loads[1].wait()
    loads[2].wait()
    frame = lax.broadcasted_iota(jnp.int32, (FR_DEV, WIDTH), 0)

    def fir(i, lanes):
        now = x[i, :, lanes].astype(jnp.float32)
        before = jnp.where(frame >= 1, pltpu.roll(now, 1, 0), 0.0)
        older = pltpu.roll(w[2:3, lanes] * now + w[3:4, lanes] * before, 2, 0)
        return w[0:1, lanes] * now + w[1:2, lanes] * before + jnp.where(frame >= 2, older, 0.0)

    for chunk in range(HALF // WIDTH):
        low = pl.ds(chunk * WIDTH, WIDTH)
        high = pl.ds(HALF + chunk * WIDTH, WIDTH)
        for i in range(IN_DEV):
            first, second = fir(i, low), fir(i, high)
            edge_ref[i, :, low] = first[:EDGE]
            edge_ref[i, :, high] = second[:EDGE]
            filt_ref[0, i * FR_DEV : (i + 1) * FR_DEV, low] = (first + second).astype(jnp.bfloat16)
            filt_ref[1, i * FR_DEV : (i + 1) * FR_DEV, low] = (first - second).astype(jnp.bfloat16)
    loads[3].wait()


def spectra_kernel(prev_ref, w_ref, pick_ref, filt_ref, edge_ref, tab_ref, out_ref, ext, filt, spec, picked, rows):
    ext[:, :EDGE, :] = jnp.zeros((IN_DEV, EDGE, POINTS), jnp.float32)
    ext[:, EDGE:, :] = jnp.zeros((IN_DEV, EDGE, POINTS), jnp.float32)
    ext[:, EDGE - (TAPS - 1) : EDGE, :] = prev_ref[...].astype(jnp.float32)

    def fir(i, lanes):
        total = edge_ref[i, :, lanes]
        for tap in range(1, TAPS):
            total = total + w_ref[tap : tap + 1, lanes] * ext[i, EDGE - tap : 2 * EDGE - tap, lanes]
        return total

    for parity in range(2):
        filt[parity] = filt_ref[parity]
        for i in range(IN_DEV):
            first, second = fir(i, slice(0, HALF)), fir(i, slice(HALF, POINTS))
            both = first + second if parity == 0 else first - second
            filt[parity, i * FR_DEV : i * FR_DEV + EDGE, :] = both.astype(jnp.bfloat16)
        both = jnp.dot(filt[parity], tab_ref[parity], preferred_element_type=jnp.float32).astype(jnp.bfloat16)
        columns = slice(parity * PART, (parity + 1) * PART)
        for i in range(IN_DEV):
            mine = both[i * FR_DEV : (i + 1) * FR_DEV]
            spec[2 * i * FR_DEV : (2 * i + 1) * FR_DEV, columns] = mine[:, :PART]
            spec[(2 * i + 1) * FR_DEV : (2 * i + 2) * FR_DEV, columns] = mine[:, PART:]
    flip = lax.axis_index("sec") & 1
    step = 64
    lower = lax.broadcasted_iota(jnp.int32, (step, 128), 1) < 64
    for quad in range(2):
        source = spec[quad * 256 : (quad + 1) * 256, :]
        for side in range(2):
            picked[quad, side] = lax.dot_general(pick_ref[side ^ flip], source, NT, preferred_element_type=jnp.float32)
        for start in range(0, DEVS, step):
            for pair in range(2):
                a, b = (picked[quad, side, start : start + step, pair * 128 : (pair + 1) * 128] for side in range(2))
                c = (jnp.where(lower, a, pltpu.roll(b, 64, 1)), jnp.where(lower, pltpu.roll(a, 64, 1), b))
                for j in range(2):
                    rows[pl.ds(start * IN_DEV + quad * 4 + pair * 2 + j, step, stride=IN_DEV), :] = c[j]
    out_ref[...] = rows[: DEVS * IN_DEV, :].astype(jnp.bfloat16)


def cross_kernel(r_ref, vis_hbm, auto_hbm, plain, twist, out, auto, sems, auto_sem):
    tile, half = 256, 128
    row = lax.broadcasted_iota(jnp.int32, (tile, tile), 0)
    column = lax.broadcasted_iota(jnp.int32, (tile, tile), 1)
    odd = (row // FR_DEV) % 2
    turn = jnp.where(column - row == FR_DEV * (1 - 2 * odd), (2 * odd - 1).astype(jnp.float32), 0.0)
    turn = turn.astype(jnp.bfloat16)
    small_row = lax.broadcasted_iota(jnp.int32, (half, half), 0)
    small_column = lax.broadcasted_iota(jnp.int32, (half, half), 1)
    above, on_diag = small_row <= small_column, small_row == small_column
    lower = lax.broadcasted_iota(jnp.int32, (INPUTS, 128), 1) < 64

    def prepare(slot):
        for pair in range(2):
            first, second = r_ref[2 * pair + slot], r_ref[2 * pair + 1 - slot]
            plain[slot, :, pair * 128 : (pair + 1) * 128] = jnp.where(lower, first, second)
        twist[slot] = jnp.dot(plain[slot], turn, preferred_element_type=jnp.float32).astype(jnp.bfloat16)

    copies = []
    prepare(0)
    for slot in range(2):
        for start in range(0, INPUTS, tile):
            end = start + tile
            mine = slice(start, end)
            real = lax.dot_general(
                plain[slot, mine, :], plain[slot, start:, :], NT, preferred_element_type=jnp.float32
            ) * (1.0 / FRAMES)
            imag = lax.dot_general(
                twist[slot, mine, :], plain[slot, :end, :], NT, preferred_element_type=jnp.float32
            ) * (1.0 / FRAMES)
            if start > 0:
                out[slot, mine, :start] = imag[:, :start].astype(jnp.bfloat16)
            if end < INPUTS:
                out[slot, mine, end:] = real[:, tile:].astype(jnp.bfloat16)
            middle = start + half
            out[slot, start:middle, middle:end] = real[:half, half:tile].astype(jnp.bfloat16)
            out[slot, middle:end, start:middle] = imag[half:, start:middle].astype(jnp.bfloat16)
            for part in range(2):
                here = slice(start + part * half, start + (part + 1) * half)
                inner = slice(part * half, (part + 1) * half)
                block = real[inner, inner]
                out[slot, here, here] = jnp.where(above, block, imag[inner, here]).astype(jnp.bfloat16)
                auto[slot : slot + 1, here] = jnp.sum(jnp.where(on_diag, block, 0.0), axis=0, keepdims=True)
            copy = pltpu.make_async_copy(out.at[slot, mine], vis_hbm.at[slot, mine], sems.at[slot, start // tile])
            copy.start()
            copies.append(copy)
            if slot == 0 and start == 0:
                prepare(1)
    copy = pltpu.make_async_copy(auto, auto_hbm, auto_sem)
    copy.start()
    copies.append(copy)
    for copy in copies:
        copy.wait()


VMEM = pl.BlockSpec(memory_space=pltpu.VMEM)
HBM = pl.BlockSpec(memory_space=pltpu.HBM)


def in_hbm(value):
    return pltpu.with_memory_space_constraint(value, pltpu.HBM)


def shaped(*shape, dtype=jnp.bfloat16):
    return jax.ShapeDtypeStruct(shape, dtype)


def local(samples, fir_weights, channel_owner):
    last_frames = samples[:, FR_DEV - (TAPS - 1) :, :]
    previous = lax.ppermute(last_frames, "sec", [(i, i + 1) for i in range(SECS - 1)])
    pick, filtered, edge, table = pl.pallas_call(
        head_kernel,
        out_shape=(
            shaped(2, DEVS, CHANNELS),
            shaped(2, ROWS, HALF),
            shaped(IN_DEV, EDGE, POINTS, dtype=jnp.float32),
            shaped(2, HALF, CHANNELS),
        ),
        in_specs=[HBM] * 4,
        out_specs=(VMEM,) * 4,
        scratch_shapes=[
            pltpu.VMEM((CHANNELS,), jnp.int32),
            pltpu.VMEM((IN_DEV, FR_DEV, POINTS), jnp.bfloat16),
            pltpu.VMEM((TAPS, POINTS), jnp.float32),
            pltpu.VMEM((CHANNELS, CHANNELS), jnp.bfloat16),
            pltpu.VMEM((CHANNELS, CHANNELS), jnp.bfloat16),
            pltpu.SemaphoreType.DMA((4,)),
        ],
        compiler_params=pltpu.CompilerParams(vmem_limit_bytes=24 * MIB),
        cost_estimate=pl.CostEstimate(flops=2 * OWNERS * CHANNELS**2, bytes_accessed=8 * MIB, transcendentals=0),
        name="head",
    )(*(in_hbm(value) for value in (channel_owner, samples, fir_weights, jnp.asarray(dft_tables()))))
    buffer = pl.pallas_call(
        spectra_kernel,
        out_shape=shaped(DEVS * IN_DEV, 128),
        in_specs=[VMEM] * 6,
        out_specs=VMEM,
        scratch_shapes=[
            pltpu.VMEM((IN_DEV, 2 * EDGE, POINTS), jnp.float32),
            pltpu.VMEM((2, ROWS, HALF), jnp.bfloat16),
            pltpu.VMEM((2 * ROWS, CHANNELS), jnp.bfloat16),
            pltpu.VMEM((2, 2, DEVS, 256), jnp.float32),
            pltpu.VMEM((DEVS * IN_DEV + 8, 128), jnp.float32),
        ],
        compiler_params=pltpu.CompilerParams(vmem_limit_bytes=32 * MIB),
        cost_estimate=pl.CostEstimate(flops=4 * ROWS * HALF * CHANNELS, bytes_accessed=8 * MIB, transcendentals=0),
        name="spectra",
    )(previous, fir_weights, pick, filtered, edge, table)
    received = lax.all_to_all(buffer, ("sec", "inp"), split_axis=0, concat_axis=0, tiled=True)
    visibility, auto_power = pl.pallas_call(
        cross_kernel,
        out_shape=(shaped(2, INPUTS, INPUTS), shaped(2, INPUTS, dtype=jnp.float32)),
        in_specs=[VMEM],
        out_specs=(HBM, HBM),
        scratch_shapes=[
            pltpu.VMEM((2, INPUTS, 256), jnp.bfloat16),
            pltpu.VMEM((2, INPUTS, 256), jnp.bfloat16),
            pltpu.VMEM((2, INPUTS, INPUTS), jnp.bfloat16),
            pltpu.VMEM((2, INPUTS), jnp.float32),
            pltpu.SemaphoreType.DMA((2, 4)),
            pltpu.SemaphoreType.DMA(()),
        ],
        compiler_params=pltpu.CompilerParams(vmem_limit_bytes=24 * MIB),
        name="cross",
    )(received.reshape(SECS, INPUTS, 128))
    return (visibility, auto_power)


def solution(mesh):
    in_specs = (P("inp", "sec", None), P(), P())
    out_specs = (P(("inp", "sec"), None, None), P(("inp", "sec"), None))
    return jax.shard_map(local, mesh=mesh, in_specs=in_specs, out_specs=out_specs, check_vma=False)
```

```python
import math

import jax
import jax.numpy as jnp
import numpy as np
from jax import lax
from jax.experimental import pallas as pl
from jax.experimental.pallas import tpu as pltpu
from jax.sharding import PartitionSpec as P

POINTS = 2048
HALF = POINTS // 2
CHANNELS = 768
PART = CHANNELS // 2
TAPS = 4
FRAMES = 128
INPUTS = 1024
OWNERS = 128
SECS = 4
DEVS = OWNERS * SECS
IN_DEV = 8
FR_DEV = 32
ROWS = IN_DEV * FR_DEV
EDGE = 8
SPAN = FR_DEV // 2
WIDTH = 256
MIB = 1 << 20
NT = (((1,), (1,)), ((), ()))


def dft_tables():
    points = np.arange(HALF, dtype=np.int64)
    tables = []
    for parity in range(2):
        channels = np.arange(parity, CHANNELS, 2, dtype=np.int64)
        angles = (points[:, None] * channels[None, :] % POINTS) * (2.0 * math.pi / POINTS)
        tables.append(np.concatenate([np.cos(angles), -np.sin(angles)], axis=1))
    return (np.stack(tables) / math.sqrt(POINTS)).astype(jnp.bfloat16)


def as_bf16(mask):
    return mask.astype(jnp.float32).astype(jnp.bfloat16)


def channel_at(axis):
    place = lax.broadcasted_iota(jnp.int32, (CHANNELS, CHANNELS), axis)
    return jnp.where(place < PART, 2 * place, 2 * place - (CHANNELS - 1))


def pick_matrix(owner, to_place, earlier, pick_ref):
    spread = jnp.broadcast_to(owner.astype(jnp.float32), (8, CHANNELS)).astype(jnp.bfloat16)
    owner = jnp.dot(spread, to_place, preferred_element_type=jnp.float32)[:1].astype(jnp.int32)
    named = (lax.broadcasted_iota(jnp.int32, (OWNERS, CHANNELS), 0) == owner).astype(jnp.float32)
    counts = jnp.dot(named.astype(jnp.bfloat16), earlier, preferred_element_type=jnp.float32)
    rank = jnp.sum(counts * named, axis=0, keepdims=True).astype(jnp.int32)
    target = ((rank >> 1) * OWNERS + owner) * 2 + (rank & 1)
    target = jnp.where(rank < 2 * SECS, target, -1)
    for side in range(2):
        place = 2 * lax.broadcasted_iota(jnp.int32, (DEVS, CHANNELS), 0) + side
        pick_ref[side] = as_bf16(place == target)


def transform(rows, table, parity, frames, spec_refs):
    both = jnp.dot(rows, table, preferred_element_type=jnp.float32).astype(jnp.bfloat16)
    columns = slice(parity * PART, (parity + 1) * PART)
    for i in range(IN_DEV):
        for half, spec_ref in enumerate(spec_refs):
            size = min(frames, SPAN)
            mine = both[i * frames + half * SPAN : i * frames + half * SPAN + size]
            start = 2 * i * SPAN
            spec_ref[start : start + size, columns] = mine[:, :PART]
            spec_ref[start + SPAN : start + SPAN + size, columns] = mine[:, PART:]


def choose(pick_ref, spec_ref, picked_ref):
    flip = lax.axis_index("sec") & 1
    spectra = spec_ref[...]
    for side in range(2):
        picked_ref[side] = lax.dot_general(pick_ref[side ^ flip], spectra, NT, preferred_element_type=jnp.float32)


def head_kernel(
    owner_hbm, x_hbm, w_hbm, tab_hbm,
    pick_ref, spec_ref, late_ref, edge_ref, tab_ref,
    owner, x, w, filt, late_spec, to_place, earlier, sems,
):
    pairs = ((owner_hbm, owner), (x_hbm, x), (w_hbm, w), (tab_hbm, tab_ref))
    loads = [pltpu.make_async_copy(source, target, sems.at[i]) for i, (source, target) in enumerate(pairs)]
    for load in loads:
        load.start()
    to_place[...] = as_bf16(lax.broadcasted_iota(jnp.int32, (CHANNELS, CHANNELS), 0) == channel_at(1))
    earlier[...] = as_bf16(channel_at(0) < channel_at(1))
    loads[0].wait()
    pick_matrix(owner[...].reshape(1, CHANNELS), to_place[...], earlier[...], pick_ref)
    loads[1].wait()
    loads[2].wait()
    frame = lax.broadcasted_iota(jnp.int32, (FR_DEV, WIDTH), 0)

    def fir(i, lanes):
        now = x[i, :, lanes].astype(jnp.float32)
        before = jnp.where(frame >= 1, pltpu.roll(now, 1, 0), 0.0)
        older = pltpu.roll(w[2:3, lanes] * now + w[3:4, lanes] * before, 2, 0)
        return w[0:1, lanes] * now + w[1:2, lanes] * before + jnp.where(frame >= 2, older, 0.0)

    for chunk in range(HALF // WIDTH):
        low = pl.ds(chunk * WIDTH, WIDTH)
        high = pl.ds(HALF + chunk * WIDTH, WIDTH)
        for i in range(IN_DEV):
            first, second = fir(i, low), fir(i, high)
            edge_ref[i, :, low] = first[:EDGE]
            edge_ref[i, :, high] = second[:EDGE]
            filt[0, i * FR_DEV : (i + 1) * FR_DEV, low] = (first + second).astype(jnp.bfloat16)
            filt[1, i * FR_DEV : (i + 1) * FR_DEV, low] = (first - second).astype(jnp.bfloat16)
    loads[3].wait()
    for parity in range(2):
        transform(filt[parity], tab_ref[parity], parity, FR_DEV, (spec_ref, late_spec))
    choose(pick_ref, late_spec, late_ref)


def spectra_kernel(
    prev_ref, w_ref, pick_ref, spec_in, late_ref, edge_ref, tab_ref, out_ref, ext, filt, spec, early, rows
):
    spec[...] = spec_in[...]
    ext[:, :EDGE, :] = jnp.zeros((IN_DEV, EDGE, POINTS), jnp.float32)
    ext[:, EDGE:, :] = jnp.zeros((IN_DEV, EDGE, POINTS), jnp.float32)
    ext[:, EDGE - (TAPS - 1) : EDGE, :] = prev_ref[...].astype(jnp.float32)

    def fir(i, lanes):
        total = edge_ref[i, :, lanes]
        for tap in range(1, TAPS):
            total = total + w_ref[tap : tap + 1, lanes] * ext[i, EDGE - tap : 2 * EDGE - tap, lanes]
        return total

    for i in range(IN_DEV):
        first, second = fir(i, slice(0, HALF)), fir(i, slice(HALF, POINTS))
        filt[0, i * EDGE : (i + 1) * EDGE, :] = (first + second).astype(jnp.bfloat16)
        filt[1, i * EDGE : (i + 1) * EDGE, :] = (first - second).astype(jnp.bfloat16)
    for parity in range(2):
        transform(filt[parity], tab_ref[parity], parity, EDGE, (spec,))
    choose(pick_ref, spec, early)
    step = 64
    group = lax.broadcasted_iota(jnp.int32, (step, 128), 1) // (2 * SPAN)
    lower, even = group < 2, (group & 1) == 0
    for start in range(0, DEVS, step):
        span = slice(start, start + step)
        for quad in range(2):
            lanes = slice(quad * 128, (quad + 1) * 128)
            a = [source[side, span, lanes] for source in (early, late_ref) for side in range(2)]
            b = [
                jnp.where(lower, a[0], pltpu.roll(a[2], 64, 1)),
                jnp.where(lower, a[1], pltpu.roll(a[3], 64, 1)),
                jnp.where(lower, pltpu.roll(a[0], 64, 1), a[2]),
                jnp.where(lower, pltpu.roll(a[1], 64, 1), a[3]),
            ]
            c = [
                jnp.where(even, b[0], pltpu.roll(b[1], 32, 1)),
                jnp.where(even, pltpu.roll(b[0], 96, 1), b[1]),
                jnp.where(even, b[2], pltpu.roll(b[3], 32, 1)),
                jnp.where(even, pltpu.roll(b[2], 96, 1), b[3]),
            ]
            for j in range(4):
                rows[pl.ds(start * IN_DEV + quad * 4 + j, step, stride=IN_DEV), :] = c[j]
    out_ref[...] = rows[: DEVS * IN_DEV, :].astype(jnp.bfloat16)


def cross_kernel(r_ref, vis_hbm, auto_hbm, plain, twist, out, auto, sems, auto_sem):
    tile, half = 256, 128
    row = lax.broadcasted_iota(jnp.int32, (tile, tile), 0)
    column = lax.broadcasted_iota(jnp.int32, (tile, tile), 1)
    odd = (row // SPAN) % 2
    turn = jnp.where(column - row == SPAN * (1 - 2 * odd), (2 * odd - 1).astype(jnp.float32), 0.0)
    turn = turn.astype(jnp.bfloat16)
    small_row = lax.broadcasted_iota(jnp.int32, (half, half), 0)
    small_column = lax.broadcasted_iota(jnp.int32, (half, half), 1)
    above, on_diag = small_row <= small_column, small_row == small_column
    first_side = (lax.broadcasted_iota(jnp.int32, (INPUTS, 128), 1) // (2 * SPAN)) % 2 == 0

    def prepare(slot):
        for pair in range(2):
            first, second = r_ref[2 * pair + slot], r_ref[2 * pair + 1 - slot]
            plain[slot, :, pair * 128 : (pair + 1) * 128] = jnp.where(first_side, first, second)
        twist[slot] = jnp.dot(plain[slot], turn, preferred_element_type=jnp.float32).astype(jnp.bfloat16)

    copies = []
    prepare(0)
    for slot in range(2):
        for start in range(0, INPUTS, tile):
            end = start + tile
            mine = slice(start, end)
            real = lax.dot_general(
                plain[slot, mine, :], plain[slot, start:, :], NT, preferred_element_type=jnp.float32
            ) * (1.0 / FRAMES)
            imag = lax.dot_general(
                twist[slot, mine, :], plain[slot, :end, :], NT, preferred_element_type=jnp.float32
            ) * (1.0 / FRAMES)
            if start > 0:
                out[slot, mine, :start] = imag[:, :start].astype(jnp.bfloat16)
            if end < INPUTS:
                out[slot, mine, end:] = real[:, tile:].astype(jnp.bfloat16)
            middle = start + half
            out[slot, start:middle, middle:end] = real[:half, half:tile].astype(jnp.bfloat16)
            out[slot, middle:end, start:middle] = imag[half:, start:middle].astype(jnp.bfloat16)
            for part in range(2):
                here = slice(start + part * half, start + (part + 1) * half)
                inner = slice(part * half, (part + 1) * half)
                block = real[inner, inner]
                out[slot, here, here] = jnp.where(above, block, imag[inner, here]).astype(jnp.bfloat16)
                auto[slot : slot + 1, here] = jnp.sum(jnp.where(on_diag, block, 0.0), axis=0, keepdims=True)
            copy = pltpu.make_async_copy(out.at[slot, mine], vis_hbm.at[slot, mine], sems.at[slot, start // tile])
            copy.start()
            copies.append(copy)
            if slot == 0 and start == 0:
                prepare(1)
    copy = pltpu.make_async_copy(auto, auto_hbm, auto_sem)
    copy.start()
    copies.append(copy)
    for copy in copies:
        copy.wait()


VMEM = pl.BlockSpec(memory_space=pltpu.VMEM)
HBM = pl.BlockSpec(memory_space=pltpu.HBM)


def in_hbm(value):
    return pltpu.with_memory_space_constraint(value, pltpu.HBM)


def shaped(*shape, dtype=jnp.bfloat16):
    return jax.ShapeDtypeStruct(shape, dtype)


def local(samples, fir_weights, channel_owner):
    last_frames = samples[:, FR_DEV - (TAPS - 1) :, :]
    previous = lax.ppermute(last_frames, "sec", [(i, i + 1) for i in range(SECS - 1)])
    pick, spectra, late, edge, table = pl.pallas_call(
        head_kernel,
        out_shape=(
            shaped(2, DEVS, CHANNELS),
            shaped(ROWS, CHANNELS),
            shaped(2, DEVS, ROWS, dtype=jnp.float32),
            shaped(IN_DEV, EDGE, POINTS, dtype=jnp.float32),
            shaped(2, HALF, CHANNELS),
        ),
        in_specs=[HBM] * 4,
        out_specs=(VMEM,) * 5,
        scratch_shapes=[
            pltpu.VMEM((CHANNELS,), jnp.int32),
            pltpu.VMEM((IN_DEV, FR_DEV, POINTS), jnp.bfloat16),
            pltpu.VMEM((TAPS, POINTS), jnp.float32),
            pltpu.VMEM((2, ROWS, HALF), jnp.bfloat16),
            pltpu.VMEM((ROWS, CHANNELS), jnp.bfloat16),
            pltpu.VMEM((CHANNELS, CHANNELS), jnp.bfloat16),
            pltpu.VMEM((CHANNELS, CHANNELS), jnp.bfloat16),
            pltpu.SemaphoreType.DMA((4,)),
        ],
        compiler_params=pltpu.CompilerParams(vmem_limit_bytes=24 * MIB),
        cost_estimate=pl.CostEstimate(flops=2 * OWNERS * CHANNELS**2, bytes_accessed=8 * MIB, transcendentals=0),
        name="head",
    )(*(in_hbm(value) for value in (channel_owner, samples, fir_weights, jnp.asarray(dft_tables()))))
    buffer = pl.pallas_call(
        spectra_kernel,
        out_shape=shaped(DEVS * IN_DEV, 128),
        in_specs=[VMEM] * 7,
        out_specs=VMEM,
        scratch_shapes=[
            pltpu.VMEM((IN_DEV, 2 * EDGE, POINTS), jnp.float32),
            pltpu.VMEM((2, IN_DEV * EDGE, HALF), jnp.bfloat16),
            pltpu.VMEM((ROWS, CHANNELS), jnp.bfloat16),
            pltpu.VMEM((2, DEVS, ROWS), jnp.float32),
            pltpu.VMEM((DEVS * IN_DEV + 8, 128), jnp.float32),
        ],
        compiler_params=pltpu.CompilerParams(vmem_limit_bytes=32 * MIB),
        cost_estimate=pl.CostEstimate(flops=4 * ROWS * HALF * CHANNELS, bytes_accessed=8 * MIB, transcendentals=0),
        name="spectra",
    )(previous, fir_weights, pick, spectra, late, edge, table)
    received = lax.all_to_all(buffer, ("sec", "inp"), split_axis=0, concat_axis=0, tiled=True)
    visibility, auto_power = pl.pallas_call(
        cross_kernel,
        out_shape=(shaped(2, INPUTS, INPUTS), shaped(2, INPUTS, dtype=jnp.float32)),
        in_specs=[VMEM],
        out_specs=(HBM, HBM),
        scratch_shapes=[
            pltpu.VMEM((2, INPUTS, 256), jnp.bfloat16),
            pltpu.VMEM((2, INPUTS, 256), jnp.bfloat16),
            pltpu.VMEM((2, INPUTS, INPUTS), jnp.bfloat16),
            pltpu.VMEM((2, INPUTS), jnp.float32),
            pltpu.SemaphoreType.DMA((2, 4)),
            pltpu.SemaphoreType.DMA(()),
        ],
        compiler_params=pltpu.CompilerParams(vmem_limit_bytes=24 * MIB),
        name="cross",
    )(received.reshape(SECS, INPUTS, 128))
    return (visibility, auto_power)


def solution(mesh):
    in_specs = (P("inp", "sec", None), P(), P())
    out_specs = (P(("inp", "sec"), None, None), P(("inp", "sec"), None))
    return jax.shard_map(local, mesh=mesh, in_specs=in_specs, out_specs=out_specs, check_vma=False)
```

```python
import math

import jax
import jax.numpy as jnp
import numpy as np
from jax import lax
from jax.experimental import pallas as pl
from jax.experimental.pallas import tpu as pltpu
from jax.sharding import PartitionSpec as P

POINTS = 2048
HALF = POINTS // 2
CHANNELS = 768
PART = CHANNELS // 2
TAPS = 4
FRAMES = 128
INPUTS = 1024
OWNERS = 128
SECS = 4
DEVS = OWNERS * SECS
IN_DEV = 8
FR_DEV = 32
ROWS = IN_DEV * FR_DEV
EDGE = 8
SPAN = FR_DEV // 2
WIDTH = 256
MIB = 1 << 20
NT = (((1,), (1,)), ((), ()))


def dft_tables():
    points = np.arange(HALF, dtype=np.int64)
    tables = []
    for parity in range(2):
        channels = np.arange(parity, CHANNELS, 2, dtype=np.int64)
        angles = (points[:, None] * channels[None, :] % POINTS) * (2.0 * math.pi / POINTS)
        tables.append(np.concatenate([np.cos(angles), -np.sin(angles)], axis=1))
    return (np.stack(tables) / math.sqrt(POINTS)).astype(jnp.bfloat16)


def as_bf16(mask):
    return mask.astype(jnp.float32).astype(jnp.bfloat16)


def channel_at(axis):
    place = lax.broadcasted_iota(jnp.int32, (CHANNELS, CHANNELS), axis)
    return jnp.where(place < PART, 2 * place, 2 * place - (CHANNELS - 1))


def pick_matrix(owner, to_place, earlier, pick_ref):
    spread = jnp.broadcast_to(owner.astype(jnp.float32), (8, CHANNELS)).astype(jnp.bfloat16)
    owner = jnp.dot(spread, to_place, preferred_element_type=jnp.float32)[:1].astype(jnp.int32)
    named = (lax.broadcasted_iota(jnp.int32, (OWNERS, CHANNELS), 0) == owner).astype(jnp.float32)
    counts = jnp.dot(named.astype(jnp.bfloat16), earlier, preferred_element_type=jnp.float32)
    rank = jnp.sum(counts * named, axis=0, keepdims=True).astype(jnp.int32)
    target = ((rank >> 1) * OWNERS + owner) * 2 + (rank & 1)
    target = jnp.where(rank < 2 * SECS, target, -1)
    for side in range(2):
        place = 2 * lax.broadcasted_iota(jnp.int32, (DEVS, CHANNELS), 0) + side
        pick_ref[side] = as_bf16(place == target)


def transform(rows, table, parity, frames, spec_refs):
    both = jnp.dot(rows, table, preferred_element_type=jnp.float32).astype(jnp.bfloat16)
    columns = slice(parity * PART, (parity + 1) * PART)
    size = min(frames, SPAN)
    for i in range(IN_DEV):
        for half, spec_ref in enumerate(spec_refs):
            mine = both[i * frames + half * SPAN : i * frames + half * SPAN + size]
            for side in range(2):
                start = (i // 4) * 128 + ((i + 2 * half + side) % 4) * 2 * SPAN
                spec_ref[side, start : start + size, columns] = mine[:, :PART]
                spec_ref[side, start + SPAN : start + SPAN + size, columns] = mine[:, PART:]


def choose(pick_ref, spec_ref, picked_ref):
    flip = lax.axis_index("sec") & 1
    for side in range(2):
        picked_ref[side] = lax.dot_general(
            pick_ref[side ^ flip], spec_ref[side], NT, preferred_element_type=jnp.float32
        )


def head_kernel(
    owner_hbm, x_hbm, w_hbm, tab_hbm,
    pick_ref, spec_ref, late_ref, edge_ref, tab_ref,
    owner, x, w, filt, late_spec, to_place, earlier, sems,
):
    pairs = ((owner_hbm, owner), (x_hbm, x), (w_hbm, w), (tab_hbm, tab_ref))
    loads = [pltpu.make_async_copy(source, target, sems.at[i]) for i, (source, target) in enumerate(pairs)]
    for load in loads:
        load.start()
    to_place[...] = as_bf16(lax.broadcasted_iota(jnp.int32, (CHANNELS, CHANNELS), 0) == channel_at(1))
    earlier[...] = as_bf16(channel_at(0) < channel_at(1))
    loads[0].wait()
    pick_matrix(owner[...].reshape(1, CHANNELS), to_place[...], earlier[...], pick_ref)
    loads[1].wait()
    loads[2].wait()
    frame = lax.broadcasted_iota(jnp.int32, (FR_DEV, WIDTH), 0)

    def fir(i, lanes):
        now = x[i, :, lanes].astype(jnp.float32)
        before = jnp.where(frame >= 1, pltpu.roll(now, 1, 0), 0.0)
        older = pltpu.roll(w[2:3, lanes] * now + w[3:4, lanes] * before, 2, 0)
        return w[0:1, lanes] * now + w[1:2, lanes] * before + jnp.where(frame >= 2, older, 0.0)

    for chunk in range(HALF // WIDTH):
        low = pl.ds(chunk * WIDTH, WIDTH)
        high = pl.ds(HALF + chunk * WIDTH, WIDTH)
        for i in range(IN_DEV):
            first, second = fir(i, low), fir(i, high)
            edge_ref[i, :, low] = first[:EDGE]
            edge_ref[i, :, high] = second[:EDGE]
            filt[0, i * FR_DEV : (i + 1) * FR_DEV, low] = (first + second).astype(jnp.bfloat16)
            filt[1, i * FR_DEV : (i + 1) * FR_DEV, low] = (first - second).astype(jnp.bfloat16)
    loads[3].wait()
    for parity in range(2):
        transform(filt[parity], tab_ref[parity], parity, FR_DEV, (spec_ref, late_spec))
    choose(pick_ref, late_spec, late_ref)


def spectra_kernel(
    prev_ref, w_ref, pick_ref, spec_in, late_ref, edge_ref, tab_ref, out_ref, ext, filt, spec, early, rows
):
    spec[...] = spec_in[...]
    ext[:, :EDGE, :] = jnp.zeros((IN_DEV, EDGE, POINTS), jnp.float32)
    ext[:, EDGE:, :] = jnp.zeros((IN_DEV, EDGE, POINTS), jnp.float32)
    ext[:, EDGE - (TAPS - 1) : EDGE, :] = prev_ref[...].astype(jnp.float32)

    def fir(i, lanes):
        total = edge_ref[i, :, lanes]
        for tap in range(1, TAPS):
            total = total + w_ref[tap : tap + 1, lanes] * ext[i, EDGE - tap : 2 * EDGE - tap, lanes]
        return total

    for i in range(IN_DEV):
        first, second = fir(i, slice(0, HALF)), fir(i, slice(HALF, POINTS))
        filt[0, i * EDGE : (i + 1) * EDGE, :] = (first + second).astype(jnp.bfloat16)
        filt[1, i * EDGE : (i + 1) * EDGE, :] = (first - second).astype(jnp.bfloat16)
    for parity in range(2):
        transform(filt[parity], tab_ref[parity], parity, EDGE, (spec,))
    choose(pick_ref, spec, early)
    step = 64
    group = lax.broadcasted_iota(jnp.int32, (step, 128), 1) // (2 * SPAN)
    lower, even = group < 2, (group & 1) == 0
    for start in range(0, DEVS, step):
        span = slice(start, start + step)
        for quad in range(2):
            lanes = slice(quad * 128, (quad + 1) * 128)
            a = [source[side, span, lanes] for source in (early, late_ref) for side in range(2)]
            for j in range(4):
                turned = [a[(place - j) % 4] for place in range(4)]
                value = jnp.where(
                    lower, jnp.where(even, turned[0], turned[1]), jnp.where(even, turned[2], turned[3])
                )
                if j > 0:
                    value = pltpu.roll(value, 128 - 2 * SPAN * j, 1)
                rows[pl.ds(start * IN_DEV + quad * 4 + j, step, stride=IN_DEV), :] = value
    out_ref[...] = rows[: DEVS * IN_DEV, :].astype(jnp.bfloat16)


def cross_kernel(r_ref, vis_hbm, auto_hbm, plain, twist, out, auto, sems, auto_sem):
    tile, half = 256, 128
    row = lax.broadcasted_iota(jnp.int32, (tile, tile), 0)
    column = lax.broadcasted_iota(jnp.int32, (tile, tile), 1)
    odd = (row // SPAN) % 2
    turn = jnp.where(column - row == SPAN * (1 - 2 * odd), (2 * odd - 1).astype(jnp.float32), 0.0)
    turn = turn.astype(jnp.bfloat16)
    small_row = lax.broadcasted_iota(jnp.int32, (half, half), 0)
    small_column = lax.broadcasted_iota(jnp.int32, (half, half), 1)
    above, on_diag = small_row <= small_column, small_row == small_column
    first_side = (lax.broadcasted_iota(jnp.int32, (INPUTS, 128), 1) // (2 * SPAN)) % 2 == 0

    def prepare(slot):
        for pair in range(2):
            first, second = r_ref[2 * pair + slot], r_ref[2 * pair + 1 - slot]
            plain[slot, :, pair * 128 : (pair + 1) * 128] = jnp.where(first_side, first, second)
        twist[slot] = jnp.dot(plain[slot], turn, preferred_element_type=jnp.float32).astype(jnp.bfloat16)

    copies = []
    prepare(0)
    for slot in range(2):
        for start in range(0, INPUTS, tile):
            end = start + tile
            mine = slice(start, end)
            real = lax.dot_general(
                plain[slot, mine, :], plain[slot, start:, :], NT, preferred_element_type=jnp.float32
            ) * (1.0 / FRAMES)
            imag = lax.dot_general(
                twist[slot, mine, :], plain[slot, :end, :], NT, preferred_element_type=jnp.float32
            ) * (1.0 / FRAMES)
            if start > 0:
                out[slot, mine, :start] = imag[:, :start].astype(jnp.bfloat16)
            if end < INPUTS:
                out[slot, mine, end:] = real[:, tile:].astype(jnp.bfloat16)
            middle = start + half
            out[slot, start:middle, middle:end] = real[:half, half:tile].astype(jnp.bfloat16)
            out[slot, middle:end, start:middle] = imag[half:, start:middle].astype(jnp.bfloat16)
            for part in range(2):
                here = slice(start + part * half, start + (part + 1) * half)
                inner = slice(part * half, (part + 1) * half)
                block = real[inner, inner]
                out[slot, here, here] = jnp.where(above, block, imag[inner, here]).astype(jnp.bfloat16)
                auto[slot : slot + 1, here] = jnp.sum(jnp.where(on_diag, block, 0.0), axis=0, keepdims=True)
            copy = pltpu.make_async_copy(out.at[slot, mine], vis_hbm.at[slot, mine], sems.at[slot, start // tile])
            copy.start()
            copies.append(copy)
            if slot == 0 and start == 0:
                prepare(1)
    copy = pltpu.make_async_copy(auto, auto_hbm, auto_sem)
    copy.start()
    copies.append(copy)
    for copy in copies:
        copy.wait()


VMEM = pl.BlockSpec(memory_space=pltpu.VMEM)
HBM = pl.BlockSpec(memory_space=pltpu.HBM)


def in_hbm(value):
    return pltpu.with_memory_space_constraint(value, pltpu.HBM)


def shaped(*shape, dtype=jnp.bfloat16):
    return jax.ShapeDtypeStruct(shape, dtype)


def local(samples, fir_weights, channel_owner):
    last_frames = samples[:, FR_DEV - (TAPS - 1) :, :]
    previous = lax.ppermute(last_frames, "sec", [(i, i + 1) for i in range(SECS - 1)])
    pick, spectra, late, edge, table = pl.pallas_call(
        head_kernel,
        out_shape=(
            shaped(2, DEVS, CHANNELS),
            shaped(2, ROWS, CHANNELS),
            shaped(2, DEVS, ROWS, dtype=jnp.float32),
            shaped(IN_DEV, EDGE, POINTS, dtype=jnp.float32),
            shaped(2, HALF, CHANNELS),
        ),
        in_specs=[HBM] * 4,
        out_specs=(VMEM,) * 5,
        scratch_shapes=[
            pltpu.VMEM((CHANNELS,), jnp.int32),
            pltpu.VMEM((IN_DEV, FR_DEV, POINTS), jnp.bfloat16),
            pltpu.VMEM((TAPS, POINTS), jnp.float32),
            pltpu.VMEM((2, ROWS, HALF), jnp.bfloat16),
            pltpu.VMEM((2, ROWS, CHANNELS), jnp.bfloat16),
            pltpu.VMEM((CHANNELS, CHANNELS), jnp.bfloat16),
            pltpu.VMEM((CHANNELS, CHANNELS), jnp.bfloat16),
            pltpu.SemaphoreType.DMA((4,)),
        ],
        compiler_params=pltpu.CompilerParams(vmem_limit_bytes=24 * MIB),
        cost_estimate=pl.CostEstimate(flops=2 * OWNERS * CHANNELS**2, bytes_accessed=8 * MIB, transcendentals=0),
        name="head",
    )(*(in_hbm(value) for value in (channel_owner, samples, fir_weights, jnp.asarray(dft_tables()))))
    buffer = pl.pallas_call(
        spectra_kernel,
        out_shape=shaped(DEVS * IN_DEV, 128),
        in_specs=[VMEM] * 7,
        out_specs=VMEM,
        scratch_shapes=[
            pltpu.VMEM((IN_DEV, 2 * EDGE, POINTS), jnp.float32),
            pltpu.VMEM((2, IN_DEV * EDGE, HALF), jnp.bfloat16),
            pltpu.VMEM((2, ROWS, CHANNELS), jnp.bfloat16),
            pltpu.VMEM((2, DEVS, ROWS), jnp.float32),
            pltpu.VMEM((DEVS * IN_DEV + 8, 128), jnp.float32),
        ],
        compiler_params=pltpu.CompilerParams(vmem_limit_bytes=32 * MIB),
        cost_estimate=pl.CostEstimate(flops=4 * ROWS * HALF * CHANNELS, bytes_accessed=8 * MIB, transcendentals=0),
        name="spectra",
    )(previous, fir_weights, pick, spectra, late, edge, table)
    received = lax.all_to_all(buffer, ("sec", "inp"), split_axis=0, concat_axis=0, tiled=True)
    visibility, auto_power = pl.pallas_call(
        cross_kernel,
        out_shape=(shaped(2, INPUTS, INPUTS), shaped(2, INPUTS, dtype=jnp.float32)),
        in_specs=[VMEM],
        out_specs=(HBM, HBM),
        scratch_shapes=[
            pltpu.VMEM((2, INPUTS, 256), jnp.bfloat16),
            pltpu.VMEM((2, INPUTS, 256), jnp.bfloat16),
            pltpu.VMEM((2, INPUTS, INPUTS), jnp.bfloat16),
            pltpu.VMEM((2, INPUTS), jnp.float32),
            pltpu.SemaphoreType.DMA((2, 4)),
            pltpu.SemaphoreType.DMA(()),
        ],
        compiler_params=pltpu.CompilerParams(vmem_limit_bytes=24 * MIB),
        name="cross",
    )(received.reshape(SECS, INPUTS, 128))
    return (visibility, auto_power)


def solution(mesh):
    in_specs = (P("inp", "sec", None), P(), P())
    out_specs = (P(("inp", "sec"), None, None), P(("inp", "sec"), None))
    return jax.shard_map(local, mesh=mesh, in_specs=in_specs, out_specs=out_specs, check_vma=False)
```

```python
import math

import jax
import jax.numpy as jnp
import numpy as np
from jax import lax
from jax.experimental import pallas as pl
from jax.experimental.pallas import tpu as pltpu
from jax.sharding import PartitionSpec as P

POINTS = 2048
HALF = POINTS // 2
CHANNELS = 768
PART = CHANNELS // 2
TAPS = 4
FRAMES = 128
INPUTS = 1024
OWNERS = 128
SECS = 4
DEVS = OWNERS * SECS
IN_DEV = 8
FR_DEV = 32
ROWS = IN_DEV * FR_DEV
EDGE = 8
REDO = EDGE // 2
SPAN = FR_DEV // 2
WIDTH = 256
MIB = 1 << 20
NT = (((1,), (1,)), ((), ()))


def dft_tables():
    points = np.arange(HALF, dtype=np.int64)
    tables = []
    for parity in range(2):
        channels = np.arange(parity, CHANNELS, 2, dtype=np.int64)
        angles = (points[:, None] * channels[None, :] % POINTS) * (2.0 * math.pi / POINTS)
        tables.append(np.concatenate([np.cos(angles), -np.sin(angles)], axis=1))
    return (np.stack(tables) / math.sqrt(POINTS)).astype(jnp.bfloat16)


def as_bf16(mask):
    return mask.astype(jnp.float32).astype(jnp.bfloat16)


def channel_at(axis):
    place = lax.broadcasted_iota(jnp.int32, (CHANNELS, CHANNELS), axis)
    return jnp.where(place < PART, 2 * place, 2 * place - (CHANNELS - 1))


def pick_matrix(owner, to_place, earlier, pick_ref):
    spread = jnp.broadcast_to(owner.astype(jnp.float32), (8, CHANNELS)).astype(jnp.bfloat16)
    owner = jnp.dot(spread, to_place, preferred_element_type=jnp.float32)[:1].astype(jnp.int32)
    named = (lax.broadcasted_iota(jnp.int32, (OWNERS, CHANNELS), 0) == owner).astype(jnp.float32)
    counts = jnp.dot(named.astype(jnp.bfloat16), earlier, preferred_element_type=jnp.float32)
    rank = jnp.sum(counts * named, axis=0, keepdims=True).astype(jnp.int32)
    target = ((rank >> 1) * OWNERS + owner) * 2 + (rank & 1)
    target = jnp.where(rank < 2 * SECS, target, -1)
    for side in range(2):
        place = 2 * lax.broadcasted_iota(jnp.int32, (DEVS, CHANNELS), 0) + side
        pick_ref[side] = as_bf16(place == target)


def transform(rows, table):
    return jnp.dot(rows, table, preferred_element_type=jnp.float32).astype(jnp.bfloat16)


def place(both, parity, frames, spec_refs):
    columns = slice(parity * PART, (parity + 1) * PART)
    size = min(frames, SPAN)
    for i in range(IN_DEV):
        for half, spec_ref in enumerate(spec_refs):
            mine = both[i * frames + half * SPAN : i * frames + half * SPAN + size]
            for side in range(2):
                start = (i // 4) * 128 + ((i + 2 * half + side) % 4) * 2 * SPAN
                spec_ref[side, start : start + size, columns] = mine[:, :PART]
                spec_ref[side, start + SPAN : start + SPAN + size, columns] = mine[:, PART:]


def choose(pick_ref, spec_ref, picked_ref):
    flip = lax.axis_index("sec") & 1
    for side in range(2):
        picked_ref[side] = lax.dot_general(
            pick_ref[side ^ flip], spec_ref[side], NT, preferred_element_type=jnp.float32
        )


def head_kernel(
    owner_hbm, x_hbm, w_hbm, tab_hbm,
    pick_ref, spec_ref, late_ref, edge_ref, tab_ref,
    owner, x, w, filt, late_spec, to_place, earlier, sems,
):
    pairs = ((owner_hbm, owner), (x_hbm, x), (w_hbm, w), (tab_hbm, tab_ref))
    loads = [pltpu.make_async_copy(source, target, sems.at[i]) for i, (source, target) in enumerate(pairs)]
    for load in loads:
        load.start()
    to_place[...] = as_bf16(lax.broadcasted_iota(jnp.int32, (CHANNELS, CHANNELS), 0) == channel_at(1))
    earlier[...] = as_bf16(channel_at(0) < channel_at(1))
    loads[0].wait()
    pick_matrix(owner[...].reshape(1, CHANNELS), to_place[...], earlier[...], pick_ref)
    loads[1].wait()
    loads[2].wait()
    frame = lax.broadcasted_iota(jnp.int32, (FR_DEV, WIDTH), 0)

    def fir(i, lanes):
        now = x[i, :, lanes].astype(jnp.float32)
        before = jnp.where(frame >= 1, pltpu.roll(now, 1, 0), 0.0)
        older = pltpu.roll(w[2:3, lanes] * now + w[3:4, lanes] * before, 2, 0)
        return w[0:1, lanes] * now + w[1:2, lanes] * before + jnp.where(frame >= 2, older, 0.0)

    for chunk in range(HALF // WIDTH):
        low = pl.ds(chunk * WIDTH, WIDTH)
        high = pl.ds(HALF + chunk * WIDTH, WIDTH)
        for i in range(IN_DEV):
            first, second = fir(i, low), fir(i, high)
            edge_ref[i, :, low] = first[:EDGE]
            edge_ref[i, :, high] = second[:EDGE]
            filt[0, i * FR_DEV : (i + 1) * FR_DEV, low] = (first + second).astype(jnp.bfloat16)
            filt[1, i * FR_DEV : (i + 1) * FR_DEV, low] = (first - second).astype(jnp.bfloat16)
    loads[3].wait()
    for parity in range(2):
        place(transform(filt[parity], tab_ref[parity]), parity, FR_DEV, (spec_ref, late_spec))
    choose(pick_ref, late_spec, late_ref)


def spectra_kernel(
    prev_ref, w_ref, pick_ref, spec_in, late_ref, edge_ref, tab_ref, out_ref, ext, filt, spec, early, rows
):
    ext[:, EDGE - (TAPS - 1) :, :] = prev_ref[...].astype(jnp.float32)
    frame = lax.broadcasted_iota(jnp.int32, (EDGE, HALF), 0)

    def fir(i, lanes):
        halo = ext[i, :, lanes]
        total = edge_ref[i, :, lanes]
        for tap in range(1, TAPS):
            total = total + jnp.where(frame < tap, w_ref[tap : tap + 1, lanes] * pltpu.roll(halo, tap, 0), 0.0)
        return total

    for i in range(0, IN_DEV, 2):
        pair = [(fir(k, slice(0, HALF)), fir(k, slice(HALF, POINTS))) for k in (i, i + 1)]
        for parity in range(2):
            mine, other = (first + second if parity == 0 else first - second for first, second in pair)
            both = jnp.where(frame < REDO, mine, pltpu.roll(other, REDO, 0))
            filt[parity, i * REDO : (i + 2) * REDO, :] = both.astype(jnp.bfloat16)
    again = [transform(filt[parity], tab_ref[parity]) for parity in range(2)]
    spec[...] = spec_in[...]
    for parity in range(2):
        place(again[parity], parity, REDO, (spec,))
    choose(pick_ref, spec, early)
    step = 64
    group = lax.broadcasted_iota(jnp.int32, (step, 128), 1) // (2 * SPAN)
    lower, even = group < 2, (group & 1) == 0
    for start in range(0, DEVS, step):
        span = slice(start, start + step)
        for quad in range(2):
            lanes = slice(quad * 128, (quad + 1) * 128)
            a = [source[side, span, lanes] for source in (early, late_ref) for side in range(2)]
            for j in range(4):
                turned = [a[(place - j) % 4] for place in range(4)]
                value = jnp.where(
                    lower, jnp.where(even, turned[0], turned[1]), jnp.where(even, turned[2], turned[3])
                )
                if j > 0:
                    value = pltpu.roll(value, 128 - 2 * SPAN * j, 1)
                rows[pl.ds(start * IN_DEV + quad * 4 + j, step, stride=IN_DEV), :] = value
    out_ref[...] = rows[: DEVS * IN_DEV, :].astype(jnp.bfloat16)


def cross_kernel(r_ref, vis_hbm, auto_hbm, plain, twist, out, auto, sems, auto_sem):
    tile, half = 256, 128
    row = lax.broadcasted_iota(jnp.int32, (tile, tile), 0)
    column = lax.broadcasted_iota(jnp.int32, (tile, tile), 1)
    odd = (row // SPAN) % 2
    turn = jnp.where(column - row == SPAN * (1 - 2 * odd), (2 * odd - 1).astype(jnp.float32), 0.0)
    turn = turn.astype(jnp.bfloat16)
    small_row = lax.broadcasted_iota(jnp.int32, (half, half), 0)
    small_column = lax.broadcasted_iota(jnp.int32, (half, half), 1)
    above, on_diag = small_row <= small_column, small_row == small_column
    first_side = (lax.broadcasted_iota(jnp.int32, (INPUTS, 128), 1) // (2 * SPAN)) % 2 == 0

    def prepare(slot):
        for pair in range(2):
            first, second = r_ref[2 * pair + slot], r_ref[2 * pair + 1 - slot]
            plain[slot, :, pair * 128 : (pair + 1) * 128] = jnp.where(first_side, first, second)
        twist[slot] = jnp.dot(plain[slot], turn, preferred_element_type=jnp.float32).astype(jnp.bfloat16)

    copies = []
    prepare(0)
    for slot in range(2):
        for start in range(0, INPUTS, tile):
            end = start + tile
            mine = slice(start, end)
            real = lax.dot_general(
                plain[slot, mine, :], plain[slot, start:, :], NT, preferred_element_type=jnp.float32
            ) * (1.0 / FRAMES)
            imag = lax.dot_general(
                twist[slot, mine, :], plain[slot, :end, :], NT, preferred_element_type=jnp.float32
            ) * (1.0 / FRAMES)
            if start > 0:
                out[slot, mine, :start] = imag[:, :start].astype(jnp.bfloat16)
            if end < INPUTS:
                out[slot, mine, end:] = real[:, tile:].astype(jnp.bfloat16)
            middle = start + half
            out[slot, start:middle, middle:end] = real[:half, half:tile].astype(jnp.bfloat16)
            out[slot, middle:end, start:middle] = imag[half:, start:middle].astype(jnp.bfloat16)
            for part in range(2):
                here = slice(start + part * half, start + (part + 1) * half)
                inner = slice(part * half, (part + 1) * half)
                block = real[inner, inner]
                out[slot, here, here] = jnp.where(above, block, imag[inner, here]).astype(jnp.bfloat16)
                auto[slot : slot + 1, here] = jnp.sum(jnp.where(on_diag, block, 0.0), axis=0, keepdims=True)
            copy = pltpu.make_async_copy(out.at[slot, mine], vis_hbm.at[slot, mine], sems.at[slot, start // tile])
            copy.start()
            copies.append(copy)
            if slot == 0 and start == 0:
                prepare(1)
    copy = pltpu.make_async_copy(auto, auto_hbm, auto_sem)
    copy.start()
    copies.append(copy)
    for copy in copies:
        copy.wait()


VMEM = pl.BlockSpec(memory_space=pltpu.VMEM)
HBM = pl.BlockSpec(memory_space=pltpu.HBM)


def in_hbm(value):
    return pltpu.with_memory_space_constraint(value, pltpu.HBM)


def shaped(*shape, dtype=jnp.bfloat16):
    return jax.ShapeDtypeStruct(shape, dtype)


def local(samples, fir_weights, channel_owner):
    last_frames = samples[:, FR_DEV - (TAPS - 1) :, :]
    previous = lax.ppermute(last_frames, "sec", [(i, i + 1) for i in range(SECS - 1)])
    pick, spectra, late, edge, table = pl.pallas_call(
        head_kernel,
        out_shape=(
            shaped(2, DEVS, CHANNELS),
            shaped(2, ROWS, CHANNELS),
            shaped(2, DEVS, ROWS, dtype=jnp.float32),
            shaped(IN_DEV, EDGE, POINTS, dtype=jnp.float32),
            shaped(2, HALF, CHANNELS),
        ),
        in_specs=[HBM] * 4,
        out_specs=(VMEM,) * 5,
        scratch_shapes=[
            pltpu.VMEM((CHANNELS,), jnp.int32),
            pltpu.VMEM((IN_DEV, FR_DEV, POINTS), jnp.bfloat16),
            pltpu.VMEM((TAPS, POINTS), jnp.float32),
            pltpu.VMEM((2, ROWS, HALF), jnp.bfloat16),
            pltpu.VMEM((2, ROWS, CHANNELS), jnp.bfloat16),
            pltpu.VMEM((CHANNELS, CHANNELS), jnp.bfloat16),
            pltpu.VMEM((CHANNELS, CHANNELS), jnp.bfloat16),
            pltpu.SemaphoreType.DMA((4,)),
        ],
        compiler_params=pltpu.CompilerParams(vmem_limit_bytes=24 * MIB),
        cost_estimate=pl.CostEstimate(flops=2 * OWNERS * CHANNELS**2, bytes_accessed=8 * MIB, transcendentals=0),
        name="head",
    )(*(in_hbm(value) for value in (channel_owner, samples, fir_weights, jnp.asarray(dft_tables()))))
    buffer = pl.pallas_call(
        spectra_kernel,
        out_shape=shaped(DEVS * IN_DEV, 128),
        in_specs=[VMEM] * 7,
        out_specs=VMEM,
        scratch_shapes=[
            pltpu.VMEM((IN_DEV, EDGE, POINTS), jnp.float32),
            pltpu.VMEM((2, IN_DEV * REDO, HALF), jnp.bfloat16),
            pltpu.VMEM((2, ROWS, CHANNELS), jnp.bfloat16),
            pltpu.VMEM((2, DEVS, ROWS), jnp.float32),
            pltpu.VMEM((DEVS * IN_DEV + 8, 128), jnp.float32),
        ],
        compiler_params=pltpu.CompilerParams(vmem_limit_bytes=32 * MIB),
        cost_estimate=pl.CostEstimate(flops=4 * ROWS * HALF * CHANNELS, bytes_accessed=8 * MIB, transcendentals=0),
        name="spectra",
    )(previous, fir_weights, pick, spectra, late, edge, table)
    received = lax.all_to_all(buffer, ("sec", "inp"), split_axis=0, concat_axis=0, tiled=True)
    visibility, auto_power = pl.pallas_call(
        cross_kernel,
        out_shape=(shaped(2, INPUTS, INPUTS), shaped(2, INPUTS, dtype=jnp.float32)),
        in_specs=[VMEM],
        out_specs=(HBM, HBM),
        scratch_shapes=[
            pltpu.VMEM((2, INPUTS, 256), jnp.bfloat16),
            pltpu.VMEM((2, INPUTS, 256), jnp.bfloat16),
            pltpu.VMEM((2, INPUTS, INPUTS), jnp.bfloat16),
            pltpu.VMEM((2, INPUTS), jnp.float32),
            pltpu.SemaphoreType.DMA((2, 4)),
            pltpu.SemaphoreType.DMA(()),
        ],
        compiler_params=pltpu.CompilerParams(vmem_limit_bytes=24 * MIB),
        name="cross",
    )(received.reshape(SECS, INPUTS, 128))
    return (visibility, auto_power)


def solution(mesh):
    in_specs = (P("inp", "sec", None), P(), P())
    out_specs = (P(("inp", "sec"), None, None), P(("inp", "sec"), None))
    return jax.shard_map(local, mesh=mesh, in_specs=in_specs, out_specs=out_specs, check_vma=False)
```

```python
import math

import jax
import jax.numpy as jnp
import numpy as np
from jax import lax
from jax.experimental import pallas as pl
from jax.experimental.pallas import tpu as pltpu
from jax.sharding import PartitionSpec as P

POINTS = 2048
HALF = POINTS // 2
CHANNELS = 768
PART = CHANNELS // 2
TAPS = 4
FRAMES = 128
INPUTS = 1024
OWNERS = 128
SECS = 4
DEVS = OWNERS * SECS
IN_DEV = 8
FR_DEV = 32
ROWS = IN_DEV * FR_DEV
EDGE = 8
REDO = EDGE // 2
SPAN = FR_DEV // 2
WIDTH = 256
MIB = 1 << 20
NT = (((1,), (1,)), ((), ()))


def dft_tables():
    points = np.arange(HALF, dtype=np.int64)
    tables = []
    for parity in range(2):
        channels = np.arange(parity, CHANNELS, 2, dtype=np.int64)
        angles = (points[:, None] * channels[None, :] % POINTS) * (2.0 * math.pi / POINTS)
        tables.append(np.concatenate([np.cos(angles), -np.sin(angles)], axis=1))
    return (np.stack(tables) / math.sqrt(POINTS)).astype(jnp.bfloat16)


def as_bf16(mask):
    return mask.astype(jnp.float32).astype(jnp.bfloat16)


def channel_at(axis):
    place = lax.broadcasted_iota(jnp.int32, (CHANNELS, CHANNELS), axis)
    return jnp.where(place < PART, 2 * place, 2 * place - (CHANNELS - 1))


def pick_matrix(owner, to_place, earlier, pick_ref):
    spread = jnp.broadcast_to(owner.astype(jnp.float32), (8, CHANNELS)).astype(jnp.bfloat16)
    owner = jnp.dot(spread, to_place, preferred_element_type=jnp.float32)[:1].astype(jnp.int32)
    named = (lax.broadcasted_iota(jnp.int32, (OWNERS, CHANNELS), 0) == owner).astype(jnp.float32)
    counts = jnp.dot(named.astype(jnp.bfloat16), earlier, preferred_element_type=jnp.float32)
    rank = jnp.sum(counts * named, axis=0, keepdims=True).astype(jnp.int32)
    target = ((rank >> 1) * OWNERS + owner) * 2 + (rank & 1)
    target = jnp.where(rank < 2 * SECS, target, -1)
    for side in range(2):
        place = 2 * lax.broadcasted_iota(jnp.int32, (DEVS, CHANNELS), 0) + side
        pick_ref[side] = as_bf16(place == target)


def transform(rows, table):
    return jnp.dot(rows, table, preferred_element_type=jnp.float32).astype(jnp.bfloat16)


def place(both, parity, frames, spec_refs):
    columns = slice(parity * PART, (parity + 1) * PART)
    size = min(frames, SPAN)
    for i in range(IN_DEV):
        for half, spec_ref in enumerate(spec_refs):
            mine = both[i * frames + half * SPAN : i * frames + half * SPAN + size]
            for side in range(2):
                start = (i // 4) * 128 + ((i + 2 * half + side) % 4) * 2 * SPAN
                spec_ref[side, start : start + size, columns] = mine[:, :PART]
                spec_ref[side, start + SPAN : start + SPAN + size, columns] = mine[:, PART:]


def choose(pick_ref, spec_ref, picked_ref):
    flip = lax.axis_index("sec") & 1
    for side in range(2):
        picked_ref[side] = lax.dot_general(
            pick_ref[side ^ flip], spec_ref[side], NT, preferred_element_type=jnp.float32
        )


def head_kernel(
    owner_hbm, x_hbm, w_hbm, tab_hbm,
    pick_ref, spec_ref, late_ref, edge_ref, tab_ref,
    owner, x, w, filt, late_spec, to_place, earlier, sems,
):
    pairs = ((owner_hbm, owner), (x_hbm, x), (w_hbm, w), (tab_hbm, tab_ref))
    loads = [pltpu.make_async_copy(source, target, sems.at[i]) for i, (source, target) in enumerate(pairs)]
    for load in loads:
        load.start()
    to_place[...] = as_bf16(lax.broadcasted_iota(jnp.int32, (CHANNELS, CHANNELS), 0) == channel_at(1))
    earlier[...] = as_bf16(channel_at(0) < channel_at(1))
    loads[0].wait()
    pick_matrix(owner[...].reshape(1, CHANNELS), to_place[...], earlier[...], pick_ref)
    loads[1].wait()
    loads[2].wait()
    frame = lax.broadcasted_iota(jnp.int32, (FR_DEV, WIDTH), 0)

    def fir(i, lanes):
        now = x[i, :, lanes].astype(jnp.float32)
        before = jnp.where(frame >= 1, pltpu.roll(now, 1, 0), 0.0)
        older = pltpu.roll(w[2:3, lanes] * now + w[3:4, lanes] * before, 2, 0)
        return w[0:1, lanes] * now + w[1:2, lanes] * before + jnp.where(frame >= 2, older, 0.0)

    for chunk in range(HALF // WIDTH):
        low = pl.ds(chunk * WIDTH, WIDTH)
        high = pl.ds(HALF + chunk * WIDTH, WIDTH)
        for i in range(IN_DEV):
            first, second = fir(i, low), fir(i, high)
            edge_ref[i, :, low] = first[:EDGE]
            edge_ref[i, :, high] = second[:EDGE]
            filt[0, i * FR_DEV : (i + 1) * FR_DEV, low] = (first + second).astype(jnp.bfloat16)
            filt[1, i * FR_DEV : (i + 1) * FR_DEV, low] = (first - second).astype(jnp.bfloat16)
    loads[3].wait()
    for parity in range(2):
        place(transform(filt[parity], tab_ref[parity]), parity, FR_DEV, (spec_ref, late_spec))
    choose(pick_ref, late_spec, late_ref)


def spectra_kernel(
    prev_ref, w_ref, pick_ref, spec_in, late_ref, edge_ref, tab_ref, out_ref, ext, filt, spec, early, rows
):
    for k in range(TAPS - 1):
        frames = prev_ref[k].astype(jnp.float32)
        for tile in range(POINTS // 128):
            at = pl.ds(EDGE - (TAPS - 1) + k, IN_DEV, stride=EDGE)
            ext[tile, at, :] = frames[:, tile * 128 : (tile + 1) * 128]
    frame = lax.broadcasted_iota(jnp.int32, (EDGE, HALF), 0)

    def fir(i, lanes):
        span = slice(i * EDGE, (i + 1) * EDGE)
        halo = jnp.concatenate([ext[tile, span, :] for tile in range(lanes.start // 128, lanes.stop // 128)], axis=1)
        total = edge_ref[i, :, lanes]
        for tap in range(1, TAPS):
            total = total + jnp.where(frame < tap, w_ref[tap : tap + 1, lanes] * pltpu.roll(halo, tap, 0), 0.0)
        return total

    for i in range(0, IN_DEV, 2):
        pair = [(fir(k, slice(0, HALF)), fir(k, slice(HALF, POINTS))) for k in (i, i + 1)]
        for parity in range(2):
            mine, other = (first + second if parity == 0 else first - second for first, second in pair)
            both = jnp.where(frame < REDO, mine, pltpu.roll(other, REDO, 0))
            filt[parity, i * REDO : (i + 2) * REDO, :] = both.astype(jnp.bfloat16)
    again = [transform(filt[parity], tab_ref[parity]) for parity in range(2)]
    spec[...] = spec_in[...]
    for parity in range(2):
        place(again[parity], parity, REDO, (spec,))
    choose(pick_ref, spec, early)
    step = 64
    group = lax.broadcasted_iota(jnp.int32, (step, 128), 1) // (2 * SPAN)
    lower, even = group < 2, (group & 1) == 0
    for start in range(0, DEVS, step):
        span = slice(start, start + step)
        for quad in range(2):
            lanes = slice(quad * 128, (quad + 1) * 128)
            a = [source[side, span, lanes] for source in (early, late_ref) for side in range(2)]
            for j in range(4):
                turned = [a[(place - j) % 4] for place in range(4)]
                value = jnp.where(
                    lower, jnp.where(even, turned[0], turned[1]), jnp.where(even, turned[2], turned[3])
                )
                if j > 0:
                    value = pltpu.roll(value, 128 - 2 * SPAN * j, 1)
                rows[pl.ds(start * IN_DEV + quad * 4 + j, step, stride=IN_DEV), :] = value
    out_ref[...] = rows[: DEVS * IN_DEV, :].astype(jnp.bfloat16)


def cross_kernel(r_ref, vis_hbm, auto_hbm, plain, twist, out, auto, sems, auto_sem):
    tile, half = 256, 128
    row = lax.broadcasted_iota(jnp.int32, (tile, tile), 0)
    column = lax.broadcasted_iota(jnp.int32, (tile, tile), 1)
    odd = (row // SPAN) % 2
    turn = jnp.where(column - row == SPAN * (1 - 2 * odd), (2 * odd - 1).astype(jnp.float32), 0.0)
    turn = turn.astype(jnp.bfloat16)
    small_row = lax.broadcasted_iota(jnp.int32, (half, half), 0)
    small_column = lax.broadcasted_iota(jnp.int32, (half, half), 1)
    above, on_diag = small_row <= small_column, small_row == small_column
    first_side = (lax.broadcasted_iota(jnp.int32, (INPUTS, 128), 1) // (2 * SPAN)) % 2 == 0

    def prepare(slot):
        for pair in range(2):
            first, second = r_ref[2 * pair + slot], r_ref[2 * pair + 1 - slot]
            plain[slot, :, pair * 128 : (pair + 1) * 128] = jnp.where(first_side, first, second)
        twist[slot] = jnp.dot(plain[slot], turn, preferred_element_type=jnp.float32).astype(jnp.bfloat16)

    copies = []
    prepare(0)
    for slot in range(2):
        for start in range(0, INPUTS, tile):
            end = start + tile
            mine = slice(start, end)
            real = lax.dot_general(
                plain[slot, mine, :], plain[slot, start:, :], NT, preferred_element_type=jnp.float32
            ) * (1.0 / FRAMES)
            imag = lax.dot_general(
                twist[slot, mine, :], plain[slot, :end, :], NT, preferred_element_type=jnp.float32
            ) * (1.0 / FRAMES)
            if start > 0:
                out[slot, mine, :start] = imag[:, :start].astype(jnp.bfloat16)
            if end < INPUTS:
                out[slot, mine, end:] = real[:, tile:].astype(jnp.bfloat16)
            middle = start + half
            out[slot, start:middle, middle:end] = real[:half, half:tile].astype(jnp.bfloat16)
            out[slot, middle:end, start:middle] = imag[half:, start:middle].astype(jnp.bfloat16)
            for part in range(2):
                here = slice(start + part * half, start + (part + 1) * half)
                inner = slice(part * half, (part + 1) * half)
                block = real[inner, inner]
                out[slot, here, here] = jnp.where(above, block, imag[inner, here]).astype(jnp.bfloat16)
                auto[slot : slot + 1, here] = jnp.sum(jnp.where(on_diag, block, 0.0), axis=0, keepdims=True)
            copy = pltpu.make_async_copy(out.at[slot, mine], vis_hbm.at[slot, mine], sems.at[slot, start // tile])
            copy.start()
            copies.append(copy)
            if slot == 0 and start == 0:
                prepare(1)
    copy = pltpu.make_async_copy(auto, auto_hbm, auto_sem)
    copy.start()
    copies.append(copy)
    for copy in copies:
        copy.wait()


VMEM = pl.BlockSpec(memory_space=pltpu.VMEM)
HBM = pl.BlockSpec(memory_space=pltpu.HBM)


def in_hbm(value):
    return pltpu.with_memory_space_constraint(value, pltpu.HBM)


def shaped(*shape, dtype=jnp.bfloat16):
    return jax.ShapeDtypeStruct(shape, dtype)


def local(samples, fir_weights, channel_owner):
    last_frames = samples[:, FR_DEV - (TAPS - 1) :, :].transpose(1, 0, 2)
    previous = lax.ppermute(last_frames, "sec", [(i, i + 1) for i in range(SECS - 1)])
    pick, spectra, late, edge, table = pl.pallas_call(
        head_kernel,
        out_shape=(
            shaped(2, DEVS, CHANNELS),
            shaped(2, ROWS, CHANNELS),
            shaped(2, DEVS, ROWS, dtype=jnp.float32),
            shaped(IN_DEV, EDGE, POINTS, dtype=jnp.float32),
            shaped(2, HALF, CHANNELS),
        ),
        in_specs=[HBM] * 4,
        out_specs=(VMEM,) * 5,
        scratch_shapes=[
            pltpu.VMEM((CHANNELS,), jnp.int32),
            pltpu.VMEM((IN_DEV, FR_DEV, POINTS), jnp.bfloat16),
            pltpu.VMEM((TAPS, POINTS), jnp.float32),
            pltpu.VMEM((2, ROWS, HALF), jnp.bfloat16),
            pltpu.VMEM((2, ROWS, CHANNELS), jnp.bfloat16),
            pltpu.VMEM((CHANNELS, CHANNELS), jnp.bfloat16),
            pltpu.VMEM((CHANNELS, CHANNELS), jnp.bfloat16),
            pltpu.SemaphoreType.DMA((4,)),
        ],
        compiler_params=pltpu.CompilerParams(vmem_limit_bytes=24 * MIB),
        cost_estimate=pl.CostEstimate(flops=2 * OWNERS * CHANNELS**2, bytes_accessed=8 * MIB, transcendentals=0),
        name="head",
    )(*(in_hbm(value) for value in (channel_owner, samples, fir_weights, jnp.asarray(dft_tables()))))
    buffer = pl.pallas_call(
        spectra_kernel,
        out_shape=shaped(DEVS * IN_DEV, 128),
        in_specs=[VMEM] * 7,
        out_specs=VMEM,
        scratch_shapes=[
            pltpu.VMEM((POINTS // 128, IN_DEV * EDGE + EDGE, 128), jnp.float32),
            pltpu.VMEM((2, IN_DEV * REDO, HALF), jnp.bfloat16),
            pltpu.VMEM((2, ROWS, CHANNELS), jnp.bfloat16),
            pltpu.VMEM((2, DEVS, ROWS), jnp.float32),
            pltpu.VMEM((DEVS * IN_DEV + 8, 128), jnp.float32),
        ],
        compiler_params=pltpu.CompilerParams(vmem_limit_bytes=32 * MIB),
        cost_estimate=pl.CostEstimate(flops=4 * ROWS * HALF * CHANNELS, bytes_accessed=8 * MIB, transcendentals=0),
        name="spectra",
    )(previous, fir_weights, pick, spectra, late, edge, table)
    received = lax.all_to_all(buffer, ("sec", "inp"), split_axis=0, concat_axis=0, tiled=True)
    visibility, auto_power = pl.pallas_call(
        cross_kernel,
        out_shape=(shaped(2, INPUTS, INPUTS), shaped(2, INPUTS, dtype=jnp.float32)),
        in_specs=[VMEM],
        out_specs=(HBM, HBM),
        scratch_shapes=[
            pltpu.VMEM((2, INPUTS, 256), jnp.bfloat16),
            pltpu.VMEM((2, INPUTS, 256), jnp.bfloat16),
            pltpu.VMEM((2, INPUTS, INPUTS), jnp.bfloat16),
            pltpu.VMEM((2, INPUTS), jnp.float32),
            pltpu.SemaphoreType.DMA((2, 4)),
            pltpu.SemaphoreType.DMA(()),
        ],
        compiler_params=pltpu.CompilerParams(vmem_limit_bytes=24 * MIB),
        name="cross",
    )(received.reshape(SECS, INPUTS, 128))
    return (visibility, auto_power)


def solution(mesh):
    in_specs = (P("inp", "sec", None), P(), P())
    out_specs = (P(("inp", "sec"), None, None), P(("inp", "sec"), None))
    return jax.shard_map(local, mesh=mesh, in_specs=in_specs, out_specs=out_specs, check_vma=False)
```

```python
import math

import jax
import jax.numpy as jnp
import numpy as np
from jax import lax
from jax.experimental import pallas as pl
from jax.experimental.pallas import tpu as pltpu
from jax.sharding import PartitionSpec as P

POINTS = 2048
HALF = POINTS // 2
CHANNELS = 768
PART = CHANNELS // 2
TAPS = 4
FRAMES = 128
INPUTS = 1024
OWNERS = 128
SECS = 4
DEVS = OWNERS * SECS
IN_DEV = 8
FR_DEV = 32
ROWS = IN_DEV * FR_DEV
EDGE = 8
REDO = EDGE // 2
SPAN = FR_DEV // 2
WIDTH = 256
MIB = 1 << 20
NT = (((1,), (1,)), ((), ()))


def dft_tables():
    points = np.arange(HALF, dtype=np.int64)
    tables = []
    for parity in range(2):
        channels = np.arange(parity, CHANNELS, 2, dtype=np.int64)
        angles = (points[:, None] * channels[None, :] % POINTS) * (2.0 * math.pi / POINTS)
        tables.append(np.concatenate([np.cos(angles), -np.sin(angles)], axis=1))
    return (np.stack(tables) / math.sqrt(POINTS)).astype(jnp.bfloat16)


def as_bf16(mask):
    return mask.astype(jnp.float32).astype(jnp.bfloat16)


def channel_at(axis):
    place = lax.broadcasted_iota(jnp.int32, (CHANNELS, CHANNELS), axis)
    return jnp.where(place < PART, 2 * place, 2 * place - (CHANNELS - 1))


def pick_matrix(owner, to_place, earlier, pick_ref):
    spread = jnp.broadcast_to(owner.astype(jnp.float32), (8, CHANNELS)).astype(jnp.bfloat16)
    owner = jnp.dot(spread, to_place, preferred_element_type=jnp.float32)[:1].astype(jnp.int32)
    named = (lax.broadcasted_iota(jnp.int32, (OWNERS, CHANNELS), 0) == owner).astype(jnp.float32)
    counts = jnp.dot(named.astype(jnp.bfloat16), earlier, preferred_element_type=jnp.float32)
    rank = jnp.sum(counts * named, axis=0, keepdims=True).astype(jnp.int32)
    device = jnp.where(rank < 2 * SECS, (rank >> 1) * OWNERS + owner, -1)
    place = lax.broadcasted_iota(jnp.int32, (DEVS, CHANNELS), 0)
    for side in range(2):
        pick_ref[side] = as_bf16(place == jnp.where((rank & 1) == side, device, -1))


def transform(rows, table):
    return jnp.dot(rows, table, preferred_element_type=jnp.float32).astype(jnp.bfloat16)


def place(both, parity, frames, spec_refs):
    columns = slice(parity * PART, (parity + 1) * PART)
    size = min(frames, SPAN)
    for i in range(IN_DEV):
        for half, spec_ref in enumerate(spec_refs):
            mine = both[i * frames + half * SPAN : i * frames + half * SPAN + size]
            for side in range(2):
                start = (i // 4) * 128 + ((i + 2 * half + side) % 4) * 2 * SPAN
                spec_ref[side, start : start + size, columns] = mine[:, :PART]
                spec_ref[side, start + SPAN : start + SPAN + size, columns] = mine[:, PART:]


def choose(pick_ref, spec_ref, picked_ref):
    flip = lax.axis_index("sec") & 1
    for side in range(2):
        picked_ref[side] = lax.dot_general(
            pick_ref[side ^ flip], spec_ref[side], NT, preferred_element_type=jnp.float32
        )


def head_kernel(
    owner_hbm, x_hbm, w_hbm, tab_hbm,
    pick_ref, spec_ref, late_ref, edge_ref, tab_ref,
    owner, x, w, filt, late_spec, to_place, earlier, sems,
):
    pairs = ((owner_hbm, owner), (x_hbm, x), (w_hbm, w), (tab_hbm, tab_ref))
    loads = [pltpu.make_async_copy(source, target, sems.at[i]) for i, (source, target) in enumerate(pairs)]
    for load in loads:
        load.start()
    to_place[...] = as_bf16(lax.broadcasted_iota(jnp.int32, (CHANNELS, CHANNELS), 0) == channel_at(1))
    earlier[...] = as_bf16(channel_at(0) < channel_at(1))
    loads[0].wait()
    pick_matrix(owner[...].reshape(1, CHANNELS), to_place[...], earlier[...], pick_ref)
    loads[1].wait()
    loads[2].wait()
    frame = lax.broadcasted_iota(jnp.int32, (FR_DEV, WIDTH), 0)

    def fir(i, lanes):
        now = x[i, :, lanes].astype(jnp.float32)
        before = jnp.where(frame >= 1, pltpu.roll(now, 1, 0), 0.0)
        older = pltpu.roll(w[2:3, lanes] * now + w[3:4, lanes] * before, 2, 0)
        return w[0:1, lanes] * now + w[1:2, lanes] * before + jnp.where(frame >= 2, older, 0.0)

    for chunk in range(HALF // WIDTH):
        low = pl.ds(chunk * WIDTH, WIDTH)
        high = pl.ds(HALF + chunk * WIDTH, WIDTH)
        for i in range(IN_DEV):
            first, second = fir(i, low), fir(i, high)
            edge_ref[i, :, low] = first[:EDGE]
            edge_ref[i, :, high] = second[:EDGE]
            filt[0, i * FR_DEV : (i + 1) * FR_DEV, low] = (first + second).astype(jnp.bfloat16)
            filt[1, i * FR_DEV : (i + 1) * FR_DEV, low] = (first - second).astype(jnp.bfloat16)
    loads[3].wait()
    for parity in range(2):
        place(transform(filt[parity], tab_ref[parity]), parity, FR_DEV, (spec_ref, late_spec))
    choose(pick_ref, late_spec, late_ref)


def spectra_kernel(
    prev_ref, w_ref, pick_ref, spec_in, late_ref, edge_ref, tab_ref, out_ref, ext, filt, spec, early, rows
):
    for k in range(TAPS - 1):
        frames = prev_ref[k].astype(jnp.float32)
        for tile in range(POINTS // 128):
            at = pl.ds(EDGE - (TAPS - 1) + k, IN_DEV, stride=EDGE)
            ext[tile, at, :] = frames[:, tile * 128 : (tile + 1) * 128]
    frame = lax.broadcasted_iota(jnp.int32, (EDGE, HALF), 0)

    def fir(i, lanes):
        span = slice(i * EDGE, (i + 1) * EDGE)
        halo = jnp.concatenate([ext[tile, span, :] for tile in range(lanes.start // 128, lanes.stop // 128)], axis=1)
        total = edge_ref[i, :, lanes]
        for tap in range(1, TAPS):
            total = total + jnp.where(frame < tap, w_ref[tap : tap + 1, lanes] * pltpu.roll(halo, tap, 0), 0.0)
        return total

    for i in range(0, IN_DEV, 2):
        pair = [(fir(k, slice(0, HALF)), fir(k, slice(HALF, POINTS))) for k in (i, i + 1)]
        for parity in range(2):
            mine, other = (first + second if parity == 0 else first - second for first, second in pair)
            both = jnp.where(frame < REDO, mine, pltpu.roll(other, REDO, 0))
            filt[parity, i * REDO : (i + 2) * REDO, :] = both.astype(jnp.bfloat16)
    again = [transform(filt[parity], tab_ref[parity]) for parity in range(2)]
    spec[...] = spec_in[...]
    for parity in range(2):
        place(again[parity], parity, REDO, (spec,))
    choose(pick_ref, spec, early)
    step = 64
    group = lax.broadcasted_iota(jnp.int32, (step, 128), 1) // (2 * SPAN)
    lower, even = group < 2, (group & 1) == 0
    for start in range(0, DEVS, step):
        span = slice(start, start + step)
        for quad in range(2):
            lanes = slice(quad * 128, (quad + 1) * 128)
            a = [source[side, span, lanes] for source in (early, late_ref) for side in range(2)]
            for j in range(4):
                turned = [a[(place - j) % 4] for place in range(4)]
                value = jnp.where(
                    lower, jnp.where(even, turned[0], turned[1]), jnp.where(even, turned[2], turned[3])
                )
                if j > 0:
                    value = pltpu.roll(value, 128 - 2 * SPAN * j, 1)
                rows[pl.ds(start * IN_DEV + quad * 4 + j, step, stride=IN_DEV), :] = value
    out_ref[...] = rows[: DEVS * IN_DEV, :].astype(jnp.bfloat16)


def cross_kernel(r_ref, vis_hbm, auto_hbm, plain, twist, out, auto, sems, auto_sem):
    tile, half = 256, 128
    row = lax.broadcasted_iota(jnp.int32, (tile, tile), 0)
    column = lax.broadcasted_iota(jnp.int32, (tile, tile), 1)
    odd = (row // SPAN) % 2
    turn = jnp.where(column - row == SPAN * (1 - 2 * odd), (2 * odd - 1).astype(jnp.float32), 0.0)
    turn = turn.astype(jnp.bfloat16)
    small_row = lax.broadcasted_iota(jnp.int32, (half, half), 0)
    small_column = lax.broadcasted_iota(jnp.int32, (half, half), 1)
    above, on_diag = small_row <= small_column, small_row == small_column
    first_side = (lax.broadcasted_iota(jnp.int32, (INPUTS, 128), 1) // (2 * SPAN)) % 2 == 0

    def prepare(slot):
        for pair in range(2):
            first, second = r_ref[2 * pair + slot], r_ref[2 * pair + 1 - slot]
            plain[slot, :, pair * 128 : (pair + 1) * 128] = jnp.where(first_side, first, second)
        twist[slot] = jnp.dot(plain[slot], turn, preferred_element_type=jnp.float32).astype(jnp.bfloat16)

    copies = []
    prepare(0)
    for slot in range(2):
        for start in range(0, INPUTS, tile):
            end = start + tile
            mine = slice(start, end)
            real = lax.dot_general(
                plain[slot, mine, :], plain[slot, start:, :], NT, preferred_element_type=jnp.float32
            ) * (1.0 / FRAMES)
            imag = lax.dot_general(
                twist[slot, mine, :], plain[slot, :end, :], NT, preferred_element_type=jnp.float32
            ) * (1.0 / FRAMES)
            if start > 0:
                out[slot, mine, :start] = imag[:, :start].astype(jnp.bfloat16)
            if end < INPUTS:
                out[slot, mine, end:] = real[:, tile:].astype(jnp.bfloat16)
            middle = start + half
            out[slot, start:middle, middle:end] = real[:half, half:tile].astype(jnp.bfloat16)
            out[slot, middle:end, start:middle] = imag[half:, start:middle].astype(jnp.bfloat16)
            for part in range(2):
                here = slice(start + part * half, start + (part + 1) * half)
                inner = slice(part * half, (part + 1) * half)
                block = real[inner, inner]
                out[slot, here, here] = jnp.where(above, block, imag[inner, here]).astype(jnp.bfloat16)
                auto[slot : slot + 1, here] = jnp.sum(jnp.where(on_diag, block, 0.0), axis=0, keepdims=True)
            copy = pltpu.make_async_copy(out.at[slot, mine], vis_hbm.at[slot, mine], sems.at[slot, start // tile])
            copy.start()
            copies.append(copy)
            if slot == 0 and start == 0:
                prepare(1)
    copy = pltpu.make_async_copy(auto, auto_hbm, auto_sem)
    copy.start()
    copies.append(copy)
    for copy in copies:
        copy.wait()


VMEM = pl.BlockSpec(memory_space=pltpu.VMEM)
HBM = pl.BlockSpec(memory_space=pltpu.HBM)


def in_hbm(value):
    return pltpu.with_memory_space_constraint(value, pltpu.HBM)


def shaped(*shape, dtype=jnp.bfloat16):
    return jax.ShapeDtypeStruct(shape, dtype)


def local(samples, fir_weights, channel_owner):
    last_frames = samples[:, FR_DEV - (TAPS - 1) :, :].transpose(1, 0, 2)
    previous = lax.ppermute(last_frames, "sec", [(i, i + 1) for i in range(SECS - 1)])
    pick, spectra, late, edge, table = pl.pallas_call(
        head_kernel,
        out_shape=(
            shaped(2, DEVS, CHANNELS),
            shaped(2, ROWS, CHANNELS),
            shaped(2, DEVS, ROWS, dtype=jnp.float32),
            shaped(IN_DEV, EDGE, POINTS, dtype=jnp.float32),
            shaped(2, HALF, CHANNELS),
        ),
        in_specs=[HBM] * 4,
        out_specs=(VMEM,) * 5,
        scratch_shapes=[
            pltpu.VMEM((CHANNELS,), jnp.int32),
            pltpu.VMEM((IN_DEV, FR_DEV, POINTS), jnp.bfloat16),
            pltpu.VMEM((TAPS, POINTS), jnp.float32),
            pltpu.VMEM((2, ROWS, HALF), jnp.bfloat16),
            pltpu.VMEM((2, ROWS, CHANNELS), jnp.bfloat16),
            pltpu.VMEM((CHANNELS, CHANNELS), jnp.bfloat16),
            pltpu.VMEM((CHANNELS, CHANNELS), jnp.bfloat16),
            pltpu.SemaphoreType.DMA((4,)),
        ],
        compiler_params=pltpu.CompilerParams(vmem_limit_bytes=24 * MIB),
        cost_estimate=pl.CostEstimate(flops=2 * OWNERS * CHANNELS**2, bytes_accessed=8 * MIB, transcendentals=0),
        name="head",
    )(*(in_hbm(value) for value in (channel_owner, samples, fir_weights, jnp.asarray(dft_tables()))))
    buffer = pl.pallas_call(
        spectra_kernel,
        out_shape=shaped(DEVS * IN_DEV, 128),
        in_specs=[VMEM] * 7,
        out_specs=VMEM,
        scratch_shapes=[
            pltpu.VMEM((POINTS // 128, IN_DEV * EDGE + EDGE, 128), jnp.float32),
            pltpu.VMEM((2, IN_DEV * REDO, HALF), jnp.bfloat16),
            pltpu.VMEM((2, ROWS, CHANNELS), jnp.bfloat16),
            pltpu.VMEM((2, DEVS, ROWS), jnp.float32),
            pltpu.VMEM((DEVS * IN_DEV + 8, 128), jnp.float32),
        ],
        compiler_params=pltpu.CompilerParams(vmem_limit_bytes=32 * MIB),
        cost_estimate=pl.CostEstimate(flops=4 * ROWS * HALF * CHANNELS, bytes_accessed=8 * MIB, transcendentals=0),
        name="spectra",
    )(previous, fir_weights, pick, spectra, late, edge, table)
    received = lax.all_to_all(buffer, ("sec", "inp"), split_axis=0, concat_axis=0, tiled=True)
    visibility, auto_power = pl.pallas_call(
        cross_kernel,
        out_shape=(shaped(2, INPUTS, INPUTS), shaped(2, INPUTS, dtype=jnp.float32)),
        in_specs=[VMEM],
        out_specs=(HBM, HBM),
        scratch_shapes=[
            pltpu.VMEM((2, INPUTS, 256), jnp.bfloat16),
            pltpu.VMEM((2, INPUTS, 256), jnp.bfloat16),
            pltpu.VMEM((2, INPUTS, INPUTS), jnp.bfloat16),
            pltpu.VMEM((2, INPUTS), jnp.float32),
            pltpu.SemaphoreType.DMA((2, 4)),
            pltpu.SemaphoreType.DMA(()),
        ],
        compiler_params=pltpu.CompilerParams(vmem_limit_bytes=24 * MIB),
        name="cross",
    )(received.reshape(SECS, INPUTS, 128))
    return (visibility, auto_power)


def solution(mesh):
    in_specs = (P("inp", "sec", None), P(), P())
    out_specs = (P(("inp", "sec"), None, None), P(("inp", "sec"), None))
    return jax.shard_map(local, mesh=mesh, in_specs=in_specs, out_specs=out_specs, check_vma=False)
```
